32 devices in a mesh: node: 8 (over z, x), tm: 4 (over y, core).
Axes of the slice: x: 2, y: 2, z: 4, core: 2. Of those that a mesh axis runs over, the one named last changes fastest.
Arguments:
- codes: int32 [32768, 512], P('node', 'tm'), may hold values from -127 to 127
- node_scale: float32 [32768], P('node'), may hold values from 0.002 to 0.02
- basis: bfloat16 [32768, 128], P('node'), may hold values from -0.03125 to 0.03125
- regular: float32 [8384], replicated, may hold values from 0.05 to 0.5
- feature_order: int32 [8384], replicated, may hold values from 0 to 8383, each once
- panel_inverse: float32 [2, 262, 262], replicated, may hold values from -0.06 to 1.2
Outputs:
- schur: float32 [8384, 8384], P('node', 'tm')
The draws below stay inside these ranges and needn't reach their ends.
Inputs may be any that keep to these rules, and one draw needn't show every extreme that they name: `feature_order`: a permutation: every feature stands at exactly one position.
All inputs are finite; a program needn't handle non-finite values.
Results may differ from the reference program's by a relative error of at most 0.0051.
Values sent between devices are 32-bit elements; how exact they have to be, the bound alone decides.
No kernel may reach another device: no remote copies, remote signals or barrier semaphores. Data moves between devices by JAX's collectives and lax.ppermute only.
A program may use at most 64 MiB of HBM per device.

```python
import math
import jax
import jax.numpy as jnp
import numpy as np
from jax import lax

RANK = 128
PW = 262
PANELS = 2
NODE_DEV = 4096
NFEAT = 8384
NODES = 32768
SNAPS = 512
N_NODE = 8


def draw_panel_inverse(key, part):
    key_off = jax.random.fold_in(key, 11)
    key_diag = jax.random.fold_in(key, 12)
    offdiag = jnp.clip(0.045 * jax.random.normal(key_off, (PANELS, PW, PW), jnp.float32), -0.06, 0.06)
    diagonal = 0.6 + 0.6 * jax.random.uniform(key_diag, (PANELS, PW), jnp.float32)
    symmetric = 0.5 * (offdiag + jnp.swapaxes(offdiag, 1, 2))
    identity = jnp.eye(PW, dtype=jnp.float32)
    return symmetric * (1.0 - identity) + diagonal[:, :, None] * identity


def plant(result, own_key, smallest, largest):
    longest = result.shape.index(max(result.shape))
    spots = []
    for shift in (0, 1):
        where = [jax.random.randint(jax.random.fold_in(own_key, axis), (), 0, length) for axis, length in enumerate(result.shape)]
        where[longest] = (where[longest] + shift) % result.shape[longest]
        spots.append(tuple(where))
    return result.at[spots[0]].set(smallest).at[spots[1]].set(largest)


def shard_levels(own_key, extent, cuts, least, high):
    level, own = 1.0, jax.random.fold_in(own_key, 6)
    for position, blocks in cuts:
        heights = jnp.exp(jax.random.uniform(jax.random.fold_in(own, position), (blocks,), jnp.float32, least / len(cuts), high / len(cuts)))
        level = level * jnp.repeat(heights, extent[position] // blocks).reshape([-1 if axis == position else 1 for axis in range(len(extent))])
    return level


def gaussian(own_key, extent, scale, bound, split=(), held_as=jnp.bfloat16):
    drawn = scale * jax.random.normal(own_key, extent, jnp.float32)
    if split:
        drawn = drawn * shard_levels(own_key, extent, split, -0.22, 0.18)
    return jnp.clip(drawn, -bound, bound).astype(held_as)


def setup_inputs(seed: int = 0) -> dict:
    splits = jax.random.split(jax.random.key(seed), 7)
    codes = plant(jax.random.randint(splits[0], (NODES, SNAPS), -127, 128), jax.random.fold_in(splits[0], 1), -127, 127).astype(jnp.int32)
    node_scale = jnp.clip(jnp.exp(math.log(0.02) - 2.30258502 * jax.random.uniform(splits[1], (NODES,), jnp.float32) ** shard_levels(splits[1], (NODES,), ((0, 8),), -0.2, 0.2)), 0.002, 0.02)
    basis = gaussian(splits[2], (NODES, RANK), NODES ** -0.5, 0.03125, ((0, 8),))
    regular = jnp.clip(jnp.exp(jax.random.uniform(splits[3], (NFEAT,), jnp.float32, math.log(0.05), math.log(0.5))), 0.05, 0.5)
    feature_order = jax.random.permutation(splits[4], NFEAT).astype(jnp.int32)
    panel_inverse = draw_panel_inverse(jax.random.fold_in(splits[6], 71), 0)
    return dict(codes=codes, node_scale=node_scale, basis=basis, regular=regular, feature_order=feature_order, panel_inverse=panel_inverse)


def pair_tables(rank_count):
    former_list = []
    latter_list = []
    for leading in range(rank_count + 1):
        for trailing in range(leading, rank_count + 1):
            if leading < rank_count or trailing < rank_count:
                former_list.append(leading)
                latter_list.append(trailing)
    return np.array(former_list, np.int32), np.array(latter_list, np.int32)


def reference(codes, node_scale, basis, regular, feature_order, panel_inverse):
    scaled_basis = (basis.astype(jnp.float32) * node_scale[:, None]).astype(jnp.bfloat16)
    code_blocks = codes.reshape(N_NODE, NODE_DEV, SNAPS)
    basis_blocks = scaled_basis.reshape(N_NODE, NODE_DEV, RANK)

    def project(running, blocks):
        code_block, basis_block = blocks
        added = lax.dot_general(code_block.astype(jnp.bfloat16), basis_block, (((0,), (0,)), ((), ())), preferred_element_type=jnp.float32)
        return running + added, None

    trajectories, _ = lax.scan(project, jnp.zeros((SNAPS, RANK), jnp.float32), (code_blocks, basis_blocks))
    former, latter = pair_tables(RANK)
    extended = jnp.concatenate([trajectories, jnp.ones((SNAPS, 1), jnp.float32)], axis=1)
    leading = jnp.take(jnp.asarray(former), feature_order)
    trailing = jnp.take(jnp.asarray(latter), feature_order)
    features = (jnp.take(extended, leading, axis=1) * jnp.take(extended, trailing, axis=1)).astype(jnp.bfloat16)
    gram = lax.dot_general(features, features, (((0,), (0,)), ((), ())), preferred_element_type=jnp.float32) / SNAPS
    matrix = gram + jnp.diag(regular)
    for panel in range(PANELS):
        lower = panel * PW
        left_part = matrix[:, lower:lower + PW]
        upper_part = matrix[lower:lower + PW, :]
        scaled_left = jnp.dot(left_part, panel_inverse[panel], precision=lax.Precision.HIGHEST, preferred_element_type=jnp.float32)
        matrix = matrix - jnp.dot(scaled_left, upper_part, precision=lax.Precision.HIGHEST, preferred_element_type=jnp.float32)
    return matrix
```

```python
import functools

import jax
import jax.numpy as jnp
from jax import lax
from jax.experimental import pallas as pl
from jax.experimental.pallas import tpu as pltpu
from jax.sharding import PartitionSpec as P

F32 = jnp.float32
BF16 = jnp.bfloat16
LANES = 128
VMEM_LIMIT = 56 * 1024 * 1024


def round_up(size, multiple):
    return -(-size // multiple) * multiple


def mm(left, right):
    return lax.dot_general(left, right, (((1,), (0,)), ((), ())), preferred_element_type=F32)


def mm_nt(left, right):
    return lax.dot_general(left, right, (((1,), (1,)), ((), ())), preferred_element_type=F32)


def mm_tn(left, right):
    return lax.dot_general(left, right, (((0,), (0,)), ((), ())), preferred_element_type=F32)


def project_kernel(codes_ref, scale_ref, basis_ref, out_ref):
    @pl.when(pl.program_id(0) == 0)
    def _():
        out_ref[...] = jnp.zeros_like(out_ref)

    modes = basis_ref[...].astype(F32).T * scale_ref[...]
    out_ref[...] += mm(modes.astype(BF16), codes_ref[...].astype(F32).astype(BF16))


def project(codes, node_scale, basis):
    nodes, snaps = codes.shape
    rank = basis.shape[1]
    block = 1024 if nodes % 1024 == 0 else nodes
    return pl.pallas_call(
        project_kernel,
        grid=(nodes // block,),
        in_specs=[
            pl.BlockSpec((block, snaps), lambda i: (i, 0)),
            pl.BlockSpec((1, block), lambda i: (0, i)),
            pl.BlockSpec((block, rank), lambda i: (i, 0)),
        ],
        out_specs=pl.BlockSpec((rank, snaps), lambda i: (0, 0)),
        out_shape=jax.ShapeDtypeStruct((rank, snaps), F32),
        name="project",
    )(codes, node_scale.reshape(1, nodes), basis)


def starts(index, rank):
    return (index * (2 * rank + 3 - index)) // 2


def decode(order, rank):
    modes = lax.broadcasted_iota(jnp.int32, (rank, order.shape[1]), 0)
    first = starts(modes, rank)
    reached = first <= order
    leading = jnp.sum(reached.astype(jnp.int32), axis=0, keepdims=True) - 1
    trailing = order - jnp.max(jnp.where(reached, first - modes, 0), axis=0, keepdims=True)
    return leading, jnp.where(order < 0, -1, trailing)


def prepare_kernel(rank, rows_ref, cols_ref, diag_ref, lead_r, trail_r, one_r, lead_c, trail_c, one_c, diag_col):
    def column(row):
        return jnp.broadcast_to(row, (LANES, row.shape[1])).T

    count = rows_ref.shape[1]
    leading, trailing = decode(rows_ref[...], rank)
    leading, trailing = column(leading.astype(F32)), column(trailing.astype(F32))
    lane = lax.broadcasted_iota(jnp.int32, (count, LANES), 1).astype(F32)
    lead_r[...] = (leading == lane).astype(F32).astype(BF16)
    trail_r[...] = (trailing == lane).astype(F32).astype(BF16)
    one_r[...] = (trailing == float(rank)).astype(F32)
    leading, trailing = decode(cols_ref[...], rank)
    mode = lax.broadcasted_iota(jnp.int32, (rank, cols_ref.shape[1]), 0)
    lead_c[...] = (leading == mode).astype(F32).astype(BF16)
    trail_c[...] = (trailing == mode).astype(F32).astype(BF16)
    one_c[...] = (trailing == rank).astype(F32)
    diag_col[...] = column(diag_ref[...])


def prepare(order_rows, order_cols, diag_panel, rank):
    rows, cols, diag = order_rows.shape[1], order_cols.shape[1], diag_panel.shape[1]
    return pl.pallas_call(
        functools.partial(prepare_kernel, rank),
        out_shape=[
            jax.ShapeDtypeStruct((rows, rank), BF16),
            jax.ShapeDtypeStruct((rows, rank), BF16),
            jax.ShapeDtypeStruct((rows, LANES), F32),
            jax.ShapeDtypeStruct((rank, cols), BF16),
            jax.ShapeDtypeStruct((rank, cols), BF16),
            jax.ShapeDtypeStruct((1, cols), F32),
            jax.ShapeDtypeStruct((diag, LANES), F32),
        ],
        compiler_params=pltpu.CompilerParams(vmem_limit_bytes=VMEM_LIMIT),
        cost_estimate=pl.CostEstimate(flops=6_000_000, bytes_accessed=4_000_000, transcendentals=0),
        name="prepare",
    )(order_rows, order_cols, diag_panel)


def split(values):
    upper = values.astype(BF16)
    return upper, (values - upper.astype(F32)).astype(BF16)


def eliminate_kernel(size, *refs):
    parts, refs = refs[: size.parts], refs[size.parts :]
    (where, lead_r, trail_r, one_r, lead_c, trail_c, one_c, diag_col, inverse, diag_panel, diag_cols) = refs[:11]
    (out_ref, modes2, modes2_t, feats_p, feats_r, weights, scaled, scaled16, schur_q) = refs[11:]
    step = pl.program_id(0)
    snaps, block = size.snaps, size.block
    inv_snaps = 1.0 / size.snaps

    def row_features(start, count):
        lead = lead_r[pl.ds(start, count), :]
        trail = trail_r[pl.ds(start, count), :]
        one = one_r[pl.ds(start, count), :]
        both = modes2_t[...]
        former = mm(jnp.concatenate([lead, lead], axis=1), both)
        latter = mm(jnp.concatenate([trail, trail], axis=1), both)
        return (former * (latter + jnp.concatenate([one] * (snaps // LANES), axis=1))).astype(BF16)

    @pl.when(step == 0)
    def _():
        modes_t = jnp.concatenate([part[...] for part in parts], axis=1)
        modes2_t[...] = jnp.concatenate(split(modes_t), axis=0)
        modes2[...] = jnp.concatenate(split(modes_t.T), axis=1)
        pad, chunk = size.panel_pad, size.chunk
        for start in range(0, 2 * pad, pad):
            feats_p[pl.ds(start, pad), :] = row_features(size.rows_pad + start, pad)
        first, second = feats_p[pl.ds(0, pad), :], feats_p[pl.ds(pad, pad), :]
        inv0, inv1 = inverse[0], inverse[1]
        inv0_16, inv1_16 = inv0.astype(BF16), inv1.astype(BF16)
        cross = (mm_nt(first, second) * inv_snaps).astype(BF16)
        coupling = mm(inv0_16, cross).astype(BF16)
        q01 = -mm(coupling, inv1_16)
        q10 = -mm_nt(inv1_16, coupling)
        q00 = inv0 - mm_nt(q01.astype(BF16), coupling)
        top = mm(q00.astype(BF16), first) + mm(q01.astype(BF16), second)
        bottom = mm(q10.astype(BF16), first) + mm(inv1_16, second)
        joint = size.panel_width // LANES * LANES
        over = pad - joint

        def pack(upper, lower, axis):
            lead_part = lax.slice_in_dim(upper, 0, joint, axis=axis)
            shared = lax.slice_in_dim(upper, joint, pad, axis=axis) + lax.slice_in_dim(lower, 0, over, axis=axis)
            tail = lax.slice_in_dim(lower, over, pad, axis=axis)
            return jnp.concatenate([lead_part, shared, tail], axis=axis)

        packed = pack(top, bottom, 0) * inv_snaps
        scaled[...] = packed
        scaled16[...] = jnp.zeros_like(scaled16)
        scaled16[pl.ds(0, size.packed), :] = packed.astype(BF16)
        schur_q[...] = jnp.zeros_like(schur_q)
        schur_q[:, pl.ds(0, size.packed)] = pack(pack(q00, q01, 1), pack(q10, inv1, 1), 0)
        spread = mm_tn(feats_p[...], jnp.concatenate([top, bottom], axis=0).astype(BF16))
        spread = (spread * inv_snaps).astype(BF16)
        for start in range(0, size.rows_feats, chunk):
            feats = row_features(start, chunk)
            feats_r[pl.ds(start, chunk), :] = feats
            weight = (feats.astype(F32) - mm(feats, spread)) * inv_snaps
            inside = min(chunk, size.packed - start)
            if inside > 0:
                own = scaled[pl.ds(start, inside), :]
                diag = jnp.concatenate([diag_col[pl.ds(start, inside), :]] * (snaps // LANES), axis=1)
                own = own * diag
                if inside < chunk:
                    own = jnp.concatenate([own, jnp.zeros((chunk - inside, snaps), F32)], axis=0)
                weight = weight - own
            weights[pl.ds(start, chunk), :] = weight.astype(BF16)

    lead, trail, both = lead_c[...], trail_c[...], modes2[...]
    former = mm(both, jnp.concatenate([lead, lead], axis=0))
    latter = mm(both, jnp.concatenate([trail, trail], axis=0)) + one_c[...]
    feats_c = (former * latter).astype(BF16)
    rows = size.rows
    product = mm(weights[...], feats_c)[:rows]
    row_id = lax.broadcasted_iota(jnp.int32, (rows, block), 0) + where[0]
    col_id = lax.broadcasted_iota(jnp.int32, (rows, block), 1) + (where[1] + step * block)
    out_ref[...] = jnp.where(row_id == col_id, product + diag_cols[...], product)

    @pl.when((where[1] == 0) & (step * block < size.panel_total))
    def _():
        at = pl.multiple_of(step * block, block)
        diag = diag_panel[:, pl.ds(at, block)]
        left = mm_nt(feats_r[...], scaled16[pl.ds(at, block), :])[:rows]
        out_ref[...] -= left * diag
        inside = min(rows, size.packed)
        own = jnp.concatenate([diag_col[pl.ds(0, inside), :]] * (block // LANES), axis=1)
        out_ref[pl.ds(0, inside), :] -= own * schur_q[pl.ds(0, inside), pl.ds(at, block)] * diag


class Sizes:
    def __init__(self, **entries):
        self.__dict__.update(entries)


def eliminate(size, parts, where, tables, inverse, diag_panel, diag_cols):
    rank, snaps, block = size.rank, size.snaps, size.block
    whole = pl.BlockSpec(memory_space=pltpu.VMEM)
    lead_r, trail_r, one_r, lead_c, trail_c, one_c, diag_col = tables
    column = lambda height: pl.BlockSpec((height, block), lambda i: (0, i))
    packed_cols = round_up(size.packed, block)
    return pl.pallas_call(
        functools.partial(eliminate_kernel, size),
        grid=(size.cols_pad // block,),
        in_specs=[whole] * size.parts
        + [pl.BlockSpec(memory_space=pltpu.SMEM)]
        + [whole] * 3
        + [column(rank), column(rank), column(1)]
        + [whole] * 3
        + [column(1)],
        out_specs=column(size.rows),
        out_shape=jax.ShapeDtypeStruct((size.rows, size.cols), F32),
        scratch_shapes=[
            pltpu.VMEM((snaps, 2 * rank), BF16),
            pltpu.VMEM((2 * rank, snaps), BF16),
            pltpu.VMEM((2 * size.panel_pad, snaps), BF16),
            pltpu.VMEM((size.rows_feats, snaps), BF16),
            pltpu.VMEM((size.rows_feats, snaps), BF16),
            pltpu.VMEM((size.packed, snaps), F32),
            pltpu.VMEM((packed_cols, snaps), BF16),
            pltpu.VMEM((size.packed, packed_cols), F32),
        ],
        compiler_params=pltpu.CompilerParams(vmem_limit_bytes=VMEM_LIMIT),
        name="eliminate",
    )(*parts, where, lead_r, trail_r, one_r, lead_c, trail_c, one_c, diag_col, inverse, diag_panel, diag_cols)


def partner(values, axis, distance):
    count = lax.axis_size(axis)
    return lax.ppermute(values, axis, [(i, i ^ distance) for i in range(count)])


def distances(axis):
    count = lax.axis_size(axis)
    assert count & (count - 1) == 0
    return [1 << bit for bit in range(count.bit_length() - 1)]


def per_device(codes, node_scale, basis, regular, feature_order, panel_inverse):
    rank = basis.shape[1]
    count = regular.shape[0]
    rows, cols = count // lax.axis_size("node"), count // lax.axis_size("tm")
    snaps = codes.shape[1] * lax.axis_size("tm")
    panels, width = panel_inverse.shape[:2]
    assert panels == 2 and panels * width <= min(rows, cols) and rank == LANES
    shift = width % LANES
    panel_pad = round_up(width + shift, LANES)
    block = 256
    size = Sizes(
        rank=rank,
        snaps=snaps,
        rows=rows,
        cols=cols,
        block=block,
        parts=lax.axis_size("tm"),
        panel_width=width,
        panel_pad=panel_pad,
        panel_total=panels * width,
        packed=width // LANES * LANES + panel_pad,
        rows_pad=round_up(rows, LANES),
        cols_pad=round_up(cols, block),
        chunk=176,
    )
    size.rows_feats = round_up(rows, size.chunk)
    row_offset = lax.axis_index("node") * rows
    col_offset = lax.axis_index("tm") * cols

    total = project(codes, node_scale, basis)

    def window(values, offset, length, padded, fill):
        taken = lax.dynamic_slice_in_dim(values, offset, length)
        return jnp.pad(taken, (0, padded - length), constant_values=fill)

    def panel_positions(values, fill):
        return [
            jnp.pad(values[:width], (0, panel_pad - width), constant_values=fill),
            jnp.pad(values[width : 2 * width], (shift, panel_pad - width - shift), constant_values=fill),
        ]

    order_rows = jnp.concatenate(
        [window(feature_order, row_offset, rows, size.rows_pad, -1)] + panel_positions(feature_order, -1)
    )
    order_cols = window(feature_order, col_offset, cols, size.cols_pad, -1)
    diag_cols = window(regular, col_offset, cols, size.cols_pad, 0)
    packed_cols = round_up(size.packed, block)
    diag_panel = jnp.pad(regular[: size.panel_total], (0, packed_cols - size.panel_total))
    diag_own = diag_panel[: size.packed] * (row_offset == 0).astype(F32)
    gaps = [(0, panel_pad - width)], [(shift, panel_pad - width - shift)]
    inverse = jnp.stack([jnp.pad(panel_inverse[k], gaps[k] * 2) for k in range(2)])
    where = jnp.stack([row_offset, col_offset]).astype(jnp.int32)
    tables = prepare(order_rows[None], order_cols[None], diag_own[None], rank)

    for distance in distances("node"):
        total = total + partner(total, "node", distance)
    parts = [total]
    for distance in reversed(distances("tm")):
        parts = parts + [partner(part, "tm", distance) for part in parts]
    return eliminate(size, parts, where, tables, inverse, diag_panel[None], diag_cols[None])


def solution(mesh):
    placed = (P("node", "tm"), P("node"), P("node", None), P(), P(), P())
    return jax.shard_map(per_device, mesh=mesh, in_specs=placed, out_specs=P("node", "tm"), check_vma=False)
```

```python
import functools

import jax
import jax.numpy as jnp
from jax import lax
from jax.experimental import pallas as pl
from jax.experimental.pallas import tpu as pltpu
from jax.sharding import PartitionSpec as P

F32 = jnp.float32
BF16 = jnp.bfloat16
LANES = 128
VMEM_LIMIT = 32 * 1024 * 1024
PREPARE_VMEM = 16 * 1024 * 1024


def round_up(size, multiple):
    return -(-size // multiple) * multiple


def mm(left, right):
    return lax.dot_general(left, right, (((1,), (0,)), ((), ())), preferred_element_type=F32)


def mm_nt(left, right):
    return lax.dot_general(left, right, (((1,), (1,)), ((), ())), preferred_element_type=F32)


def mm_tn(left, right):
    return lax.dot_general(left, right, (((0,), (0,)), ((), ())), preferred_element_type=F32)


def project_kernel(codes_ref, scale_ref, basis_ref, out_ref):
    @pl.when(pl.program_id(0) == 0)
    def _():
        out_ref[...] = jnp.zeros_like(out_ref)

    modes = basis_ref[...].astype(F32).T * scale_ref[...]
    out_ref[...] += mm(modes.astype(BF16), codes_ref[...].astype(F32).astype(BF16))


def project(codes, node_scale, basis):
    nodes, snaps = codes.shape
    rank = basis.shape[1]
    block = nodes // 2 if nodes % 2048 == 0 else nodes
    return pl.pallas_call(
        project_kernel,
        grid=(nodes // block,),
        in_specs=[
            pl.BlockSpec((block, snaps), lambda i: (i, 0)),
            pl.BlockSpec((1, block), lambda i: (0, i)),
            pl.BlockSpec((block, rank), lambda i: (i, 0)),
        ],
        out_specs=pl.BlockSpec((rank, snaps), lambda i: (0, 0)),
        out_shape=jax.ShapeDtypeStruct((rank, snaps), F32),
        name="project",
    )(codes, node_scale.reshape(1, nodes), basis)


def starts(index, rank):
    return (index * (2 * rank + 3 - index)) // 2


def decode(order, rank):
    modes = lax.broadcasted_iota(jnp.int32, (rank, order.shape[1]), 0)
    first = starts(modes, rank)
    reached = first <= order
    leading = jnp.sum(reached.astype(jnp.int32), axis=0, keepdims=True) - 1
    trailing = order - jnp.max(jnp.where(reached, first - modes, 0), axis=0, keepdims=True)
    return leading, jnp.where(order < 0, -1, trailing)


def prepare_kernel(size, rows_ref, cols_ref, diag_ref, lead_r, trail_r, one_r, lead_c, trail_c, one_c, diag_col):
    def column(row):
        return jnp.broadcast_to(row, (LANES, row.shape[1])).T

    rank, count = size.rank, lead_r.shape[0]
    leading, trailing = decode(rows_ref[:, pl.ds(0, count)], rank)
    leading, trailing = column(leading.astype(F32)), column(trailing.astype(F32))
    lane = lax.broadcasted_iota(jnp.int32, (count, LANES), 1).astype(F32)
    lead_r[...] = (leading == lane).astype(F32).astype(BF16)
    trail_r[...] = (trailing == lane).astype(F32).astype(BF16)
    one_r[...] = (trailing == float(rank)).astype(F32)
    leading, trailing = decode(cols_ref[:, pl.ds(0, size.cols_pad)], rank)
    mode = lax.broadcasted_iota(jnp.int32, (rank, size.cols_pad), 0)
    lead_c[...] = (leading == mode).astype(F32).astype(BF16)
    trail_c[...] = (trailing == mode).astype(F32).astype(BF16)
    one_c[...] = (trailing == rank).astype(F32)
    diag_col[...] = column(diag_ref[:, pl.ds(0, size.packed)])


def prepare(size, order_rows, order_cols, diag_own):
    rank, cols, rows = size.rank, size.cols_pad, size.rows_pad + 2 * size.panel_pad
    return pl.pallas_call(
        functools.partial(prepare_kernel, size),
        out_shape=[
            jax.ShapeDtypeStruct((rows, rank), BF16),
            jax.ShapeDtypeStruct((rows, rank), BF16),
            jax.ShapeDtypeStruct((rows, LANES), F32),
            jax.ShapeDtypeStruct((rank, cols), BF16),
            jax.ShapeDtypeStruct((rank, cols), BF16),
            jax.ShapeDtypeStruct((1, cols), F32),
            jax.ShapeDtypeStruct((size.packed, LANES), F32),
        ],
        compiler_params=pltpu.CompilerParams(vmem_limit_bytes=PREPARE_VMEM),
        cost_estimate=pl.CostEstimate(flops=6_000_000, bytes_accessed=4_000_000, transcendentals=0),
        name="prepare",
    )(order_rows, order_cols, diag_own)


def split(values):
    upper = values.astype(BF16)
    return upper, (values - upper.astype(F32)).astype(BF16)


def eliminate_kernel(size, *refs):
    parts, refs = refs[: size.parts], refs[size.parts :]
    (where, lead_r, trail_r, one_r, lead_c, trail_c, one_c, diag_col, inverse0, inverse1, diag_panel, diag_cols) = refs[:12]
    (out, modes2, modes2_t, feats_p, feats_r, feats_c, weights, panel_w, panel_w16, schur_q, block_sum, sems) = refs[12:]
    snaps, block, rows, cols = size.snaps, size.block, size.rows, size.cols
    pad, chunk = size.panel_pad, size.chunk
    inv_snaps = 1.0 / size.snaps

    modes_t = jnp.concatenate([part[...] for part in parts], axis=1)
    modes2_t[...] = jnp.concatenate(split(modes_t), axis=0)
    modes2[...] = jnp.concatenate(split(modes_t.T), axis=1)

    def row_features(start, count):
        lead = lead_r[pl.ds(start, count), :]
        trail = trail_r[pl.ds(start, count), :]
        one = one_r[pl.ds(start, count), :]
        both = modes2_t[...]
        former = mm(jnp.concatenate([lead, lead], axis=1), both)
        latter = mm(jnp.concatenate([trail, trail], axis=1), both)
        return (former * (latter + jnp.concatenate([one] * (snaps // LANES), axis=1))).astype(BF16)

    def column_features(start, count):
        lead = lead_c[:, pl.ds(start, count)]
        trail = trail_c[:, pl.ds(start, count)]
        both = modes2[...]
        former = mm(both, jnp.concatenate([lead, lead], axis=0))
        latter = mm(both, jnp.concatenate([trail, trail], axis=0)) + one_c[:, pl.ds(start, count)]
        feats_c[:, pl.ds(start, count)] = (former * latter).astype(BF16)

    for start in range(0, 2 * pad, pad):
        feats_p[pl.ds(start, pad), :] = row_features(size.rows_pad + start, pad)
    first, second = feats_p[pl.ds(0, pad), :], feats_p[pl.ds(pad, pad), :]
    inv0, inv1 = inverse0[...], inverse1[...]
    inv0_16, inv1_16 = inv0.astype(BF16), inv1.astype(BF16)
    fillers = [functools.partial(column_features, start, min(block, size.cols_pad - start)) for start in range(0, size.cols_pad, block)]

    def fill():
        if fillers:
            fillers.pop(0)()

    cross = (mm_nt(first, second) * inv_snaps).astype(BF16)
    fill()
    coupling = mm(inv0_16, cross).astype(BF16)
    fill()
    q01 = -mm(coupling, inv1_16)
    q10 = -mm_nt(inv1_16, coupling)
    fill()
    q00 = inv0 - mm_nt(q01.astype(BF16), coupling)
    fill()
    top = mm(q00.astype(BF16), first) + mm(q01.astype(BF16), second)
    bottom = mm(q10.astype(BF16), first) + mm(inv1_16, second)
    while fillers:
        fill()
    joint = size.panel_width // LANES * LANES
    over = pad - joint

    def pack(upper, lower, axis):
        lead_part = lax.slice_in_dim(upper, 0, joint, axis=axis)
        shared = lax.slice_in_dim(upper, joint, pad, axis=axis) + lax.slice_in_dim(lower, 0, over, axis=axis)
        tail = lax.slice_in_dim(lower, over, pad, axis=axis)
        return jnp.concatenate([lead_part, shared, tail], axis=axis)

    packed = pack(top, bottom, 0) * inv_snaps
    panel_w[...] = packed
    panel_w16[pl.ds(0, size.packed), :] = packed.astype(BF16)
    if panel_w16.shape[0] > size.packed:
        panel_w16[pl.ds(size.packed, panel_w16.shape[0] - size.packed), :] = jnp.zeros(
            (panel_w16.shape[0] - size.packed, snaps), BF16
        )
    schur_q[...] = pack(pack(q00, q01, 1), pack(q10, inv1, 1), 0)
    spread = mm_tn(feats_p[...], jnp.concatenate([top, bottom], axis=0).astype(BF16))
    spread = (spread * inv_snaps).astype(BF16)
    for start in range(0, size.rows_feats, chunk):
        feats = row_features(start, chunk)
        feats_r[pl.ds(start, chunk), :] = feats
        weight = (feats.astype(F32) - mm(feats, spread)) * inv_snaps
        inside = min(chunk, size.packed - start)
        if inside > 0:
            own = panel_w[pl.ds(start, inside), :]
            own = own * jnp.concatenate([diag_col[pl.ds(start, inside), :]] * (snaps // LANES), axis=1)
            if inside < chunk:
                own = jnp.concatenate([own, jnp.zeros((chunk - inside, snaps), F32)], axis=0)
            weight = weight - own
        weights[pl.ds(start, chunk), :] = weight.astype(BF16)

    delta = where[0] - where[1]

    def write(first_panel):
        copies = []
        for index, (start, count) in enumerate(size.row_blocks):
            kept = min(count, rows - start)
            at = pl.ds(start, kept)
            full = mm(weights[pl.ds(start, count), :], feats_c[...])[:kept, :cols]
            row_id = lax.broadcasted_iota(jnp.int32, full.shape, 0)
            col_id = lax.broadcasted_iota(jnp.int32, full.shape, 1)
            full = full + jnp.where(col_id - row_id == delta + start, diag_cols[:, pl.ds(0, cols)], 0.0)
            if first_panel:
                used = min(size.packed, cols)
                diag = diag_panel[:, pl.ds(0, used)]
                left = mm_nt(feats_r[pl.ds(start, count), :], panel_w16[...])[:kept, :used]
                inside = min(kept, size.packed - start)
                if inside > 0:
                    own = jnp.concatenate([diag_col[pl.ds(start, inside), :]] * (size.packed // LANES), axis=1)
                    own = (own * schur_q[pl.ds(start, inside), :])[:, :used]
                    if inside < kept:
                        own = jnp.concatenate([own, jnp.zeros((kept - inside, used), F32)], axis=0)
                    left = left + own
                part = full[:, :used] - left * diag
                block_sum[at, pl.ds(0, used)] = part
                if used < cols:
                    block_sum[at, pl.ds(used, cols - used)] = full[:, used:]
            else:
                block_sum[at, :] = full
            copy = pltpu.make_async_copy(block_sum.at[at, :], out.at[at, :], sems.at[index])
            copy.start()
            copies.append(copy)
        for copy in copies:
            copy.wait()

    @pl.when(where[1] == 0)
    def _():
        write(True)

    @pl.when(where[1] != 0)
    def _():
        write(False)


class Sizes:
    def __init__(self, **entries):
        self.__dict__.update(entries)


def eliminate(size, parts, where, tables, inverses, diag_panel, diag_cols):
    rank, snaps, block = size.rank, size.snaps, size.block
    whole = pl.BlockSpec(memory_space=pltpu.VMEM)
    return pl.pallas_call(
        functools.partial(eliminate_kernel, size),
        in_specs=[whole] * size.parts + [pl.BlockSpec(memory_space=pltpu.SMEM)] + [whole] * 11,
        out_specs=pl.BlockSpec(memory_space=pl.ANY),
        out_shape=jax.ShapeDtypeStruct((size.rows, size.cols), F32),
        scratch_shapes=[
            pltpu.VMEM((snaps, 2 * rank), BF16),
            pltpu.VMEM((2 * rank, snaps), BF16),
            pltpu.VMEM((2 * size.panel_pad, snaps), BF16),
            pltpu.VMEM((size.rows_feats, snaps), BF16),
            pltpu.VMEM((snaps, size.cols_pad), BF16),
            pltpu.VMEM((size.rows_feats, snaps), BF16),
            pltpu.VMEM((size.packed, snaps), F32),
            pltpu.VMEM((round_up(size.packed, LANES), snaps), BF16),
            pltpu.VMEM((size.packed, size.packed), F32),
            pltpu.VMEM((size.rows, size.cols), F32),
            pltpu.SemaphoreType.DMA((len(size.row_blocks),)),
        ],
        compiler_params=pltpu.CompilerParams(vmem_limit_bytes=VMEM_LIMIT),
        name="eliminate",
    )(*parts, where, *tables, *inverses, diag_panel, diag_cols)


def partner(values, axis, distance):
    count = lax.axis_size(axis)
    return lax.ppermute(values, axis, [(i, i ^ distance) for i in range(count)])


def distances(axis):
    count = lax.axis_size(axis)
    assert count & (count - 1) == 0
    return [1 << bit for bit in range(count.bit_length() - 1)]


def row_blocks(rows):
    return [(start, min(176, rows - start)) for start in range(0, rows, 176)]


def per_device(codes, node_scale, basis, regular, feature_order, panel_inverse):
    rank = basis.shape[1]
    count = regular.shape[0]
    rows, cols = count // lax.axis_size("node"), count // lax.axis_size("tm")
    snaps = codes.shape[1] * lax.axis_size("tm")
    panels, width = panel_inverse.shape[:2]
    assert panels == 2 and panels * width <= min(rows, cols) and rank == LANES
    shift = width % LANES
    panel_pad = round_up(width + shift, LANES)
    block = 512
    size = Sizes(
        rank=rank,
        snaps=snaps,
        rows=rows,
        cols=cols,
        block=block,
        parts=lax.axis_size("tm"),
        panel_width=width,
        panel_pad=panel_pad,
        panel_total=panels * width,
        packed=width // LANES * LANES + panel_pad,
        rows_pad=round_up(rows, LANES),
        long=1024,
        cols_pad=round_up(cols, 256),
        chunk=176,
    )
    size.rows_feats = round_up(rows, size.chunk)
    size.row_blocks = row_blocks(size.rows_feats)
    row_offset = lax.axis_index("node") * rows
    col_offset = lax.axis_index("tm") * cols

    total = project(codes, node_scale, basis)

    def window(values, offset, length, padded, fill):
        taken = lax.dynamic_slice_in_dim(values, offset, length)
        return jnp.pad(taken, (0, padded - length), constant_values=fill)

    def panel_positions(values, fill):
        return [
            jnp.pad(values[:width], (0, panel_pad - width), constant_values=fill),
            jnp.pad(values[width : 2 * width], (shift, panel_pad - width - shift), constant_values=fill),
        ]

    def long_row(values, fill):
        length = values.shape[0]
        return jnp.pad(values, (0, round_up(length, size.long) - length), constant_values=fill)[None]

    order_rows = long_row(
        jnp.concatenate(
            [window(feature_order, row_offset, rows, size.rows_pad, -1)] + panel_positions(feature_order, -1)
        ),
        -1,
    )
    order_cols = long_row(lax.dynamic_slice_in_dim(feature_order, col_offset, cols), -1)
    diag_cols = long_row(lax.dynamic_slice_in_dim(regular, col_offset, cols), 0)
    diag_panel = long_row(regular[: size.panel_total], 0)
    diag_own = diag_panel * (row_offset == 0).astype(F32)
    gaps = [(0, panel_pad - width)], [(shift, panel_pad - width - shift)]
    inverses = [jnp.pad(panel_inverse[k], gaps[k] * 2) for k in range(2)]
    where = jnp.stack([row_offset, col_offset]).astype(jnp.int32)
    inputs = (order_rows, order_cols, diag_own, diag_panel, diag_cols, inverses, where)
    tables = None
    for turn, distance in enumerate(distances("node")):
        total = total + partner(total, "node", distance)
        if turn == 0:
            total, inputs = lax.optimization_barrier((total, inputs))
            order_rows, order_cols, diag_own, diag_panel, diag_cols, inverses, where = inputs
            tables = prepare(size, order_rows, order_cols, diag_own)
        elif turn == 1:
            total, tables = lax.optimization_barrier((total, tables))
    parts = [total]
    for distance in reversed(distances("tm")):
        parts = parts + [partner(part, "tm", distance) for part in parts]
    return eliminate(size, parts, where, tables, inverses, diag_panel, diag_cols)


def solution(mesh):
    placed = (P("node", "tm"), P("node"), P("node", None), P(), P(), P())
    return jax.shard_map(per_device, mesh=mesh, in_specs=placed, out_specs=P("node", "tm"), check_vma=False)
```

```python
import functools

import jax
import jax.numpy as jnp
from jax import lax
from jax.experimental import pallas as pl
from jax.experimental.pallas import tpu as pltpu
from jax.sharding import PartitionSpec as P

F32 = jnp.float32
BF16 = jnp.bfloat16
LANES = 128
VMEM_LIMIT = 32 * 1024 * 1024
PREPARE_VMEM = 16 * 1024 * 1024
FILL = (3, 4, 4, 4)
JOIN = (0, 3, 6, 9)


def round_up(size, multiple):
    return -(-size // multiple) * multiple


def mm(left, right):
    return lax.dot_general(left, right, (((1,), (0,)), ((), ())), preferred_element_type=F32)


def mm_nt(left, right):
    return lax.dot_general(left, right, (((1,), (1,)), ((), ())), preferred_element_type=F32)


def mm_tn(left, right):
    return lax.dot_general(left, right, (((0,), (0,)), ((), ())), preferred_element_type=F32)


def project_kernel(codes_ref, scale_ref, basis_ref, out_ref):
    @pl.when(pl.program_id(0) == 0)
    def _():
        out_ref[...] = jnp.zeros_like(out_ref)

    modes = basis_ref[...].astype(F32).T * scale_ref[...]
    out_ref[...] += mm(modes.astype(BF16), codes_ref[...].astype(F32).astype(BF16))


def project(codes, node_scale, basis):
    nodes, snaps = codes.shape
    rank = basis.shape[1]
    block = nodes // 2 if nodes % 2048 == 0 else nodes
    return pl.pallas_call(
        project_kernel,
        grid=(nodes // block,),
        in_specs=[
            pl.BlockSpec((block, snaps), lambda i: (i, 0)),
            pl.BlockSpec((1, block), lambda i: (0, i)),
            pl.BlockSpec((block, rank), lambda i: (i, 0)),
        ],
        out_specs=pl.BlockSpec((rank, snaps), lambda i: (0, 0)),
        out_shape=jax.ShapeDtypeStruct((rank, snaps), F32),
        name="project",
    )(codes, node_scale.reshape(1, nodes), basis)


def starts(index, rank):
    return (index * (2 * rank + 3 - index)) // 2


def decode(order, rank):
    modes = lax.broadcasted_iota(jnp.int32, (rank, order.shape[1]), 0)
    first = starts(modes, rank)
    reached = first <= order
    leading = jnp.sum(reached.astype(jnp.int32), axis=0, keepdims=True) - 1
    trailing = order - jnp.max(jnp.where(reached, first - modes, 0), axis=0, keepdims=True)
    return leading, jnp.where(order < 0, -1, trailing)


def column(row):
    return jnp.broadcast_to(row, (LANES, row.shape[1])).T


def take_window(values, offset, length, padded, fill):
    total = round_up(values.shape[1], LANES)
    values = jnp.pad(values, ((0, 0), (0, total - values.shape[1])))
    moved = pltpu.roll(values, lax.rem(total - offset, total), 1)[:, :padded]
    lane = lax.broadcasted_iota(jnp.int32, moved.shape, 1)
    return jnp.where(lane < length, moved, fill)


def prepare_rows_kernel(size, order_ref, regular_ref, lead, trail, one, diag_col, diag_panel):
    count = lead.shape[0]
    offset = lax.axis_index("node") * size.rows
    order = order_ref[...].reshape(1, size.count)
    parts = [take_window(order, offset, size.rows, size.rows_pad, -1)]
    lane = lax.broadcasted_iota(jnp.int32, (1, size.panel_pad), 1)
    for first in (0, size.panel_width):
        tile, shift = first // LANES * LANES, first % LANES
        inside = (lane >= shift) & (lane < shift + size.panel_width)
        parts.append(jnp.where(inside, order[:, tile : tile + size.panel_pad], -1))
    leading, trailing = decode(jnp.concatenate(parts, axis=1), size.rank)
    leading, trailing = column(leading.astype(F32)), column(trailing.astype(F32))
    lane = lax.broadcasted_iota(jnp.int32, (count, LANES), 1).astype(F32)
    lead[...] = (leading == lane).astype(F32).astype(BF16)
    trail[...] = (trailing == lane).astype(F32).astype(BF16)
    one[...] = (trailing == float(size.rank)).astype(F32)
    regular = regular_ref[...].reshape(1, size.count)[:, : size.packed]
    lane = lax.broadcasted_iota(jnp.int32, regular.shape, 1)
    diag = jnp.where(lane < size.panel_total, regular, 0.0)
    diag_panel[...] = diag
    diag_col[...] = column(jnp.where(offset == 0, diag, 0.0))


def prepare_cols_kernel(size, order_ref, regular_ref, lead, trail, one, diag_cols):
    offset = lax.axis_index("tm") * size.cols
    order = take_window(order_ref[...].reshape(1, size.count), offset, size.cols, size.cols_pad, -1)
    diag_cols[...] = take_window(regular_ref[...].reshape(1, size.count), offset, size.cols, size.cols_pad, 0.0)
    leading, trailing = decode(order, size.rank)
    mode = lax.broadcasted_iota(jnp.int32, (size.rank, size.cols_pad), 0)
    lead[...] = (leading == mode).astype(F32).astype(BF16)
    trail[...] = (trailing == mode).astype(F32).astype(BF16)
    one[...] = (trailing == size.rank).astype(F32)


def prepare(kernel, name, size, shapes, feature_order, regular):
    return pl.pallas_call(
        functools.partial(kernel, size),
        in_specs=[pl.BlockSpec(memory_space=pltpu.VMEM)] * 2,
        out_shape=[jax.ShapeDtypeStruct(shape, dtype) for shape, dtype in shapes],
        compiler_params=pltpu.CompilerParams(vmem_limit_bytes=PREPARE_VMEM),
        cost_estimate=pl.CostEstimate(flops=3_000_000, bytes_accessed=2_000_000, transcendentals=0),
        name=name,
    )(feature_order, regular)


def prepare_rows(size, feature_order, regular):
    rows = size.rows_pad + 2 * size.panel_pad
    shapes = [((rows, size.rank), BF16)] * 2 + [((rows, LANES), F32)]
    shapes += [((size.packed, LANES), F32), ((1, size.packed), F32)]
    return prepare(prepare_rows_kernel, "prepare_rows", size, shapes, feature_order, regular)


def prepare_cols(size, feature_order, regular):
    shapes = [((size.rank, size.cols_pad), BF16)] * 2 + [((1, size.cols_pad), F32)] * 2
    return prepare(prepare_cols_kernel, "prepare_cols", size, shapes, feature_order, regular)


def split(values):
    upper = values.astype(BF16)
    return upper, (values - upper.astype(F32)).astype(BF16)


def eliminate_kernel(size, *refs):
    parts, refs = refs[: size.parts], refs[size.parts :]
    lead_r, trail_r, one_r, diag_col, diag_panel, lead_c, trail_c, one_c, diag_cols, inverse0, inverse1 = refs[:11]
    (out, modes2, modes2_t, feats_p, feats_r, feats_c, weights, panel_w, panel_w16, schur_q, block_sum, sems) = refs[11:]
    row_offset = lax.axis_index("node") * size.rows
    col_offset = lax.axis_index("tm") * size.cols
    snaps, block, rows, cols = size.snaps, size.block, size.rows, size.cols
    pad, chunk = size.panel_pad, size.chunk
    inv_snaps = 1.0 / size.snaps

    modes_t = jnp.concatenate([part[...] for part in parts], axis=1)
    modes2_t[...] = jnp.concatenate(split(modes_t), axis=0)
    modes2[...] = jnp.concatenate(split(modes_t.T), axis=1)

    def row_features(start, count):
        lead = lead_r[pl.ds(start, count), :]
        trail = trail_r[pl.ds(start, count), :]
        one = one_r[pl.ds(start, count), :]
        both = modes2_t[...]
        former = mm(jnp.concatenate([lead, lead], axis=1), both)
        latter = mm(jnp.concatenate([trail, trail], axis=1), both)
        return (former * (latter + jnp.concatenate([one] * (snaps // LANES), axis=1))).astype(BF16)

    def column_features(start, count):
        lead = lead_c[:, pl.ds(start, count)]
        trail = trail_c[:, pl.ds(start, count)]
        both = modes2[...]
        former = mm(both, jnp.concatenate([lead, lead], axis=0))
        latter = mm(both, jnp.concatenate([trail, trail], axis=0)) + one_c[:, pl.ds(start, count)]
        feats_c[:, pl.ds(start, count)] = (former * latter).astype(BF16)

    joint = size.panel_width // LANES * LANES
    over = pad - joint

    def pack(upper, lower, axis):
        lead_part = lax.slice_in_dim(upper, 0, joint, axis=axis)
        shared = lax.slice_in_dim(upper, joint, pad, axis=axis) + lax.slice_in_dim(lower, 0, over, axis=axis)
        tail = lax.slice_in_dim(lower, over, pad, axis=axis)
        return jnp.concatenate([lead_part, shared, tail], axis=axis)

    fillers = []

    def fill(count):
        while fillers and count > 0:
            fillers.pop(0)()
            count -= 1

    def make_rows(start):
        feats_r[pl.ds(start, chunk), :] = row_features(start, chunk)

    for start in range(0, 2 * pad, pad):
        feats_p[pl.ds(start, pad), :] = row_features(size.rows_pad + start, pad)
    for start in range(0, size.rows_feats, chunk):
        fillers.append(functools.partial(make_rows, start))
    for start in range(0, size.cols_pad, block):
        fillers.append(functools.partial(column_features, start, min(block, size.cols_pad - start)))
    first, second = feats_p[pl.ds(0, pad), :], feats_p[pl.ds(pad, pad), :]
    inv0, inv1 = inverse0[...].astype(BF16), inverse1[...].astype(BF16)
    cross = (mm_nt(second, first) * inv_snaps).astype(BF16)
    inner = {}

    def join(turn):
        if turn == 0:
            inner["coupling"] = mm_nt(inv0, cross).astype(BF16)
        elif turn == 1:
            inner["q01"] = -mm(inner["coupling"], inv1)
        elif turn == 2:
            inner["q10"] = -mm_nt(inv1, inner["coupling"])
        else:
            q00 = inverse0[...] - mm_nt(inner["q01"].astype(BF16), inner["coupling"])
            schur_q[...] = pack(pack(q00, inner["q01"], 1), pack(inner["q10"], inverse1[...], 1), 0)

    for turn, place in enumerate(JOIN):
        fillers.insert(place, functools.partial(join, turn))
    scaled0 = mm(inv0, first).astype(BF16)
    fill(FILL[0])
    left1 = (second.astype(F32) - mm(cross, scaled0)).astype(BF16)
    fill(FILL[1])
    scaled1 = mm(inv1, left1)
    fill(FILL[2])
    scaled1_16 = scaled1.astype(BF16)
    spread = mm_tn(jnp.concatenate([first, left1], axis=0), jnp.concatenate([scaled0, scaled1_16], axis=0))
    spread = (spread * inv_snaps).astype(BF16)
    fill(FILL[3])
    back = first.astype(F32) - mm_tn(cross, scaled1_16)
    packed = pack(mm(inv0, back.astype(BF16)), scaled1, 0) * inv_snaps
    panel_w[...] = packed
    panel_w16[...] = packed.astype(BF16)
    fill(len(fillers))
    for start in range(0, size.rows_feats, chunk):
        feats = feats_r[pl.ds(start, chunk), :]
        weight = (feats.astype(F32) - mm(feats, spread)) * inv_snaps
        inside = min(chunk, size.packed - start)
        if inside > 0:
            own = panel_w[pl.ds(start, inside), :]
            own = own * jnp.concatenate([diag_col[pl.ds(start, inside), :]] * (snaps // LANES), axis=1)
            if inside < chunk:
                own = jnp.concatenate([own, jnp.zeros((chunk - inside, snaps), F32)], axis=0)
            weight = weight - own
        weights[pl.ds(start, chunk), :] = weight.astype(BF16)

    delta = row_offset - col_offset

    def write(first_panel):
        copies = []
        for index, (start, count) in enumerate(size.row_blocks):
            kept = min(count, rows - start)
            at = pl.ds(start, kept)
            full = mm(weights[pl.ds(start, count), :], feats_c[...])[:kept, :cols]
            row_id = lax.broadcasted_iota(jnp.int32, full.shape, 0)
            col_id = lax.broadcasted_iota(jnp.int32, full.shape, 1)
            full = full + jnp.where(col_id - row_id == delta + start, diag_cols[:, pl.ds(0, cols)], 0.0)
            if first_panel:
                used = min(size.packed, cols)
                diag = diag_panel[:, pl.ds(0, used)]
                left = mm_nt(feats_r[pl.ds(start, count), :], panel_w16[...])[:kept, :used]
                inside = min(kept, size.packed - start)
                if inside > 0:
                    own = jnp.concatenate([diag_col[pl.ds(start, inside), :]] * (size.packed // LANES), axis=1)
                    own = (own * schur_q[pl.ds(start, inside), :])[:, :used]
                    if inside < kept:
                        own = jnp.concatenate([own, jnp.zeros((kept - inside, used), F32)], axis=0)
                    left = left + own
                part = full[:, :used] - left * diag
                block_sum[at, pl.ds(0, used)] = part
                if used < cols:
                    block_sum[at, pl.ds(used, cols - used)] = full[:, used:]
            else:
                block_sum[at, :] = full
            copy = pltpu.make_async_copy(block_sum.at[at, :], out.at[at, :], sems.at[index])
            copy.start()
            copies.append(copy)
        for copy in copies:
            copy.wait()

    @pl.when(col_offset == 0)
    def _():
        write(True)

    @pl.when(col_offset != 0)
    def _():
        write(False)


class Sizes:
    def __init__(self, **entries):
        self.__dict__.update(entries)


def eliminate(size, parts, tables, inverses):
    rank, snaps = size.rank, size.snaps
    whole = pl.BlockSpec(memory_space=pltpu.VMEM)
    return pl.pallas_call(
        functools.partial(eliminate_kernel, size),
        in_specs=[whole] * (size.parts + 11),
        out_specs=pl.BlockSpec(memory_space=pl.ANY),
        out_shape=jax.ShapeDtypeStruct((size.rows, size.cols), F32),
        scratch_shapes=[
            pltpu.VMEM((snaps, 2 * rank), BF16),
            pltpu.VMEM((2 * rank, snaps), BF16),
            pltpu.VMEM((2 * size.panel_pad, snaps), BF16),
            pltpu.VMEM((size.rows_feats, snaps), BF16),
            pltpu.VMEM((snaps, size.cols_pad), BF16),
            pltpu.VMEM((size.rows_feats, snaps), BF16),
            pltpu.VMEM((size.packed, snaps), F32),
            pltpu.VMEM((size.packed, snaps), BF16),
            pltpu.VMEM((size.packed, size.packed), F32),
            pltpu.VMEM((size.rows, size.cols), F32),
            pltpu.SemaphoreType.DMA((len(size.row_blocks),)),
        ],
        compiler_params=pltpu.CompilerParams(vmem_limit_bytes=VMEM_LIMIT),
        name="eliminate",
    )(*parts, *tables, *inverses)


def partner(values, axis, distance):
    count = lax.axis_size(axis)
    return lax.ppermute(values, axis, [(i, i ^ distance) for i in range(count)])


def distances(axis):
    count = lax.axis_size(axis)
    assert count & (count - 1) == 0
    return [1 << bit for bit in range(count.bit_length() - 1)]


def row_blocks(rows):
    return [(start, min(176, rows - start)) for start in range(0, rows, 176)]


def per_device(codes, node_scale, basis, regular, feature_order, panel_inverse):
    rank = basis.shape[1]
    count = regular.shape[0]
    rows, cols = count // lax.axis_size("node"), count // lax.axis_size("tm")
    snaps = codes.shape[1] * lax.axis_size("tm")
    panels, width = panel_inverse.shape[:2]
    assert panels == 2 and panels * width <= min(rows, cols) and rank == LANES
    shift = width % LANES
    panel_pad = round_up(width + shift, LANES)
    block = 512
    size = Sizes(
        rank=rank,
        snaps=snaps,
        rows=rows,
        cols=cols,
        block=block,
        parts=lax.axis_size("tm"),
        panel_width=width,
        panel_pad=panel_pad,
        panel_total=panels * width,
        packed=width // LANES * LANES + panel_pad,
        rows_pad=round_up(rows, LANES),
        count=count,
        cols_pad=round_up(cols, 256),
        chunk=176,
    )
    size.rows_feats = round_up(rows, size.chunk)
    size.row_blocks = row_blocks(size.rows_feats)
    total = project(codes, node_scale, basis)
    gaps = [(0, panel_pad - width)], [(shift, panel_pad - width - shift)]
    inverses = [jnp.pad(panel_inverse[k], gaps[k] * 2) for k in range(2)]

    makers = [prepare_rows, prepare_cols]
    tables = []
    for distance in distances("node"):
        total = total + partner(total, "node", distance)
        if makers:
            made = makers.pop(0)(size, feature_order, regular)
            total, made = lax.optimization_barrier((total, made))
            tables += made
    parts = [total]
    for distance in reversed(distances("tm")):
        parts = parts + [partner(part, "tm", distance) for part in parts]
    return eliminate(size, parts, tables, inverses)


def solution(mesh):
    placed = (P("node", "tm"), P("node"), P("node", None), P(), P(), P())
    return jax.shard_map(per_device, mesh=mesh, in_specs=placed, out_specs=P("node", "tm"), check_vma=False)
```

```python
import functools

import jax
import jax.numpy as jnp
from jax import lax
from jax.experimental import pallas as pl
from jax.experimental.pallas import tpu as pltpu
from jax.sharding import PartitionSpec as P

F32 = jnp.float32
BF16 = jnp.bfloat16
LANES = 128
VMEM_LIMIT = 32 * 1024 * 1024
SMALL_VMEM = 16 * 1024 * 1024
FILL = (3, 4, 4, 4)
JOIN = (0, 3, 6, 9)


def round_up(size, multiple):
    return -(-size // multiple) * multiple


def mm(left, right):
    return lax.dot_general(left, right, (((1,), (0,)), ((), ())), preferred_element_type=F32)


def mm_nt(left, right):
    return lax.dot_general(left, right, (((1,), (1,)), ((), ())), preferred_element_type=F32)


def mm_tn(left, right):
    return lax.dot_general(left, right, (((0,), (0,)), ((), ())), preferred_element_type=F32)


def in_hbm(*arrays):
    return [pltpu.with_memory_space_constraint(array, pltpu.HBM) for array in arrays]


def project_kernel(codes_ref, scale_ref, basis_ref, out_ref):
    @pl.when(pl.program_id(0) == 0)
    def _():
        out_ref[...] = jnp.zeros_like(out_ref)

    modes = basis_ref[...].astype(F32).T * scale_ref[...]
    out_ref[...] += mm(modes.astype(BF16), codes_ref[...].astype(F32).astype(BF16))


def project(codes, node_scale, basis):
    nodes, snaps = codes.shape
    rank = basis.shape[1]
    block = nodes // 2 if nodes % 2048 == 0 else nodes
    codes, scale, basis = in_hbm(codes, node_scale.reshape(1, nodes), basis)
    return pl.pallas_call(
        project_kernel,
        grid=(nodes // block,),
        in_specs=[
            pl.BlockSpec((block, snaps), lambda i: (i, 0)),
            pl.BlockSpec((1, block), lambda i: (0, i)),
            pl.BlockSpec((block, rank), lambda i: (i, 0)),
        ],
        out_specs=pl.BlockSpec((rank, snaps), lambda i: (0, 0)),
        out_shape=jax.ShapeDtypeStruct((rank, snaps), F32),
        compiler_params=pltpu.CompilerParams(vmem_limit_bytes=SMALL_VMEM),
        name="project",
    )(codes, scale, basis)


def starts(index, rank):
    return (index * (2 * rank + 3 - index)) // 2


def decode(order, rank):
    modes = lax.broadcasted_iota(jnp.int32, (rank, order.shape[1]), 0)
    first = starts(modes, rank)
    reached = first <= order
    leading = jnp.sum(reached.astype(jnp.int32), axis=0, keepdims=True) - 1
    trailing = order - jnp.max(jnp.where(reached, first - modes, 0), axis=0, keepdims=True)
    return leading, jnp.where(order < 0, -1, trailing)


def column(row):
    return jnp.broadcast_to(row, (LANES, row.shape[1])).T


def take_window(values, offset, length, padded, fill):
    total = round_up(values.shape[1], LANES)
    values = jnp.pad(values, ((0, 0), (0, total - values.shape[1])))
    moved = pltpu.roll(values, lax.rem(total - offset, total), 1)[:, :padded]
    lane = lax.broadcasted_iota(jnp.int32, moved.shape, 1)
    return jnp.where(lane < length, moved, fill)


def prepare_rows_kernel(size, order_ref, regular_ref, lead, trail, one, diag_col, diag_panel):
    count = lead.shape[0]
    offset = lax.axis_index("node") * size.rows
    order = order_ref[...].reshape(1, size.count)
    parts = [take_window(order, offset, size.rows, size.rows_pad, -1)]
    lane = lax.broadcasted_iota(jnp.int32, (1, size.panel_pad), 1)
    for first in (0, size.panel_width):
        tile, shift = first // LANES * LANES, first % LANES
        inside = (lane >= shift) & (lane < shift + size.panel_width)
        parts.append(jnp.where(inside, order[:, tile : tile + size.panel_pad], -1))
    leading, trailing = decode(jnp.concatenate(parts, axis=1), size.rank)
    leading, trailing = column(leading.astype(F32)), column(trailing.astype(F32))
    lane = lax.broadcasted_iota(jnp.int32, (count, LANES), 1).astype(F32)
    lead[...] = (leading == lane).astype(F32).astype(BF16)
    trail[...] = (trailing == lane).astype(F32).astype(BF16)
    one[...] = (trailing == float(size.rank)).astype(F32)
    regular = regular_ref[...].reshape(1, size.count)[:, : size.packed]
    lane = lax.broadcasted_iota(jnp.int32, regular.shape, 1)
    diag = jnp.where(lane < size.panel_total, regular, 0.0)
    diag_panel[...] = diag
    diag_col[...] = column(jnp.where(offset == 0, diag, 0.0))


def prepare_cols_kernel(size, order_ref, regular_ref, lead, trail, one, diag_cols):
    offset = lax.axis_index("tm") * size.cols
    order = take_window(order_ref[...].reshape(1, size.count), offset, size.cols, size.cols_pad, -1)
    diag_cols[...] = take_window(regular_ref[...].reshape(1, size.count), offset, size.cols, size.cols_pad, 0.0)
    leading, trailing = decode(order, size.rank)
    mode = lax.broadcasted_iota(jnp.int32, (size.rank, size.cols_pad), 0)
    lead[...] = (leading == mode).astype(F32).astype(BF16)
    trail[...] = (trailing == mode).astype(F32).astype(BF16)
    one[...] = (trailing == size.rank).astype(F32)


def prepare(kernel, name, size, shapes, feature_order, regular):
    return pl.pallas_call(
        functools.partial(kernel, size),
        in_specs=[pl.BlockSpec(memory_space=pltpu.VMEM)] * 2,
        out_shape=[jax.ShapeDtypeStruct(shape, dtype) for shape, dtype in shapes],
        compiler_params=pltpu.CompilerParams(vmem_limit_bytes=SMALL_VMEM),
        cost_estimate=pl.CostEstimate(flops=3_000_000, bytes_accessed=2_000_000, transcendentals=0),
        name=name,
    )(*in_hbm(feature_order, regular))


def prepare_rows(size, feature_order, regular):
    rows = size.rows_pad + 2 * size.panel_pad
    shapes = [((rows, size.rank), BF16)] * 2 + [((rows, LANES), F32)]
    shapes += [((size.packed, LANES), F32), ((1, size.packed), F32)]
    return prepare(prepare_rows_kernel, "prepare_rows", size, shapes, feature_order, regular)


def prepare_cols(size, feature_order, regular):
    shapes = [((size.rank, size.cols_pad), BF16)] * 2 + [((1, size.cols_pad), F32)] * 2
    return prepare(prepare_cols_kernel, "prepare_cols", size, shapes, feature_order, regular)


def split(values):
    upper = values.astype(BF16)
    return upper, (values - upper.astype(F32)).astype(BF16)


def feature_makers(parts, lead_r, trail_r, one_r, lead_c, trail_c, one_c):
    modes_t = jnp.concatenate([part[...] for part in parts], axis=1)
    snaps = modes_t.shape[1]
    modes2_t = jnp.concatenate(split(modes_t), axis=0)
    modes2 = jnp.concatenate(split(modes_t.T), axis=1)

    def row_features(start, count):
        lead = lead_r[pl.ds(start, count), :]
        trail = trail_r[pl.ds(start, count), :]
        one = one_r[pl.ds(start, count), :]
        former = mm(jnp.concatenate([lead, lead], axis=1), modes2_t)
        latter = mm(jnp.concatenate([trail, trail], axis=1), modes2_t)
        return (former * (latter + jnp.concatenate([one] * (snaps // LANES), axis=1))).astype(BF16)

    def column_features(start, count):
        lead = lead_c[:, pl.ds(start, count)]
        trail = trail_c[:, pl.ds(start, count)]
        former = mm(modes2, jnp.concatenate([lead, lead], axis=0))
        latter = mm(modes2, jnp.concatenate([trail, trail], axis=0)) + one_c[:, pl.ds(start, count)]
        return (former * latter).astype(BF16)

    return row_features, column_features


def features_kernel(size, *refs):
    parts, refs = refs[: size.parts], refs[size.parts :]
    tables, (feats_p, feats_r, feats_c) = refs[:6], refs[6:]
    row_features, column_features = feature_makers(parts, *tables)
    for start in range(0, 2 * size.panel_pad, size.panel_pad):
        feats_p[pl.ds(start, size.panel_pad), :] = row_features(size.rows_pad + start, size.panel_pad)
    for start in range(0, size.rows_feats, size.chunk):
        feats_r[pl.ds(start, size.chunk), :] = row_features(start, size.chunk)
    for start in range(0, size.cols_pad, size.block):
        count = min(size.block, size.cols_pad - start)
        feats_c[:, pl.ds(start, count)] = column_features(start, count)


def feature_shapes(size):
    half = size.snaps // 2
    return [(2 * size.panel_pad, half), (size.rows_feats, half), (half, size.cols_pad)]


def features(size, parts, tables):
    return pl.pallas_call(
        functools.partial(features_kernel, size),
        in_specs=[pl.BlockSpec(memory_space=pltpu.VMEM)] * (size.parts + 6),
        out_shape=[jax.ShapeDtypeStruct(shape, BF16) for shape in feature_shapes(size)],
        compiler_params=pltpu.CompilerParams(vmem_limit_bytes=SMALL_VMEM),
        cost_estimate=pl.CostEstimate(flops=1_000_000_000, bytes_accessed=2_000_000, transcendentals=0),
        name="features",
    )(*parts, *tables)


def eliminate_kernel(size, *refs):
    parts, refs = refs[: size.parts], refs[size.parts :]
    tables, refs = refs[:6], refs[6:]
    diag_col, diag_panel, diag_cols, feats_p0, feats_r0, feats_c0, inverse0, inverse1 = refs[:8]
    out, feats_p1, feats_r1, feats_c1, weights, panel_w, panel_w16, schur_q, block_sum, sems = refs[8:]
    row_offset = lax.axis_index("node") * size.rows
    col_offset = lax.axis_index("tm") * size.cols
    snaps, block, rows, cols = size.snaps, size.block, size.rows, size.cols
    pad, chunk = size.panel_pad, size.chunk
    inv_snaps = 1.0 / size.snaps
    row_features, column_features = feature_makers(parts, *tables)

    def row_block(start, count):
        at = pl.ds(start, count)
        return jnp.concatenate([feats_r0[at, :], feats_r1[at, :]], axis=1)

    joint = size.panel_width // LANES * LANES
    over = pad - joint

    def pack(upper, lower, axis):
        lead_part = lax.slice_in_dim(upper, 0, joint, axis=axis)
        shared = lax.slice_in_dim(upper, joint, pad, axis=axis) + lax.slice_in_dim(lower, 0, over, axis=axis)
        tail = lax.slice_in_dim(lower, over, pad, axis=axis)
        return jnp.concatenate([lead_part, shared, tail], axis=axis)

    fillers = []

    def fill(count):
        while fillers and count > 0:
            fillers.pop(0)()
            count -= 1

    def make_rows(start):
        feats_r1[pl.ds(start, chunk), :] = row_features(start, chunk)

    def make_columns(start, count):
        feats_c1[:, pl.ds(start, count)] = column_features(start, count)

    panels = []
    for start in range(0, 2 * pad, pad):
        at = pl.ds(start, pad)
        feats_p1[at, :] = row_features(size.rows_pad + start, pad)
        panels.append(jnp.concatenate([feats_p0[at, :], feats_p1[at, :]], axis=1))
    for start in range(0, size.rows_feats, chunk):
        fillers.append(functools.partial(make_rows, start))
    for start in range(0, size.cols_pad, block):
        fillers.append(functools.partial(make_columns, start, min(block, size.cols_pad - start)))
    first, second = panels
    inv0, inv1 = inverse0[...].astype(BF16), inverse1[...].astype(BF16)
    cross = (mm_nt(second, first) * inv_snaps).astype(BF16)
    inner = {}

    def join(turn):
        if turn == 0:
            inner["coupling"] = mm_nt(inv0, cross).astype(BF16)
        elif turn == 1:
            inner["q01"] = -mm(inner["coupling"], inv1)
        elif turn == 2:
            inner["q10"] = -mm_nt(inv1, inner["coupling"])
        else:
            q00 = inverse0[...] - mm_nt(inner["q01"].astype(BF16), inner["coupling"])
            schur_q[...] = pack(pack(q00, inner["q01"], 1), pack(inner["q10"], inverse1[...], 1), 0)

    for turn, place in enumerate(JOIN):
        fillers.insert(place, functools.partial(join, turn))
    scaled0 = mm(inv0, first).astype(BF16)
    fill(FILL[0])
    left1 = (second.astype(F32) - mm(cross, scaled0)).astype(BF16)
    fill(FILL[1])
    scaled1 = mm(inv1, left1)
    fill(FILL[2])
    scaled1_16 = scaled1.astype(BF16)
    spread = mm_tn(jnp.concatenate([first, left1], axis=0), jnp.concatenate([scaled0, scaled1_16], axis=0))
    spread = (spread * inv_snaps).astype(BF16)
    fill(FILL[3])
    back = first.astype(F32) - mm_tn(cross, scaled1_16)
    packed = pack(mm(inv0, back.astype(BF16)), scaled1, 0) * inv_snaps
    panel_w[...] = packed
    panel_w16[...] = packed.astype(BF16)
    fill(len(fillers))
    for start in range(0, size.rows_feats, chunk):
        feats = row_block(start, chunk)
        weight = (feats.astype(F32) - mm(feats, spread)) * inv_snaps
        inside = min(chunk, size.packed - start)
        if inside > 0:
            own = panel_w[pl.ds(start, inside), :]
            own = own * jnp.concatenate([diag_col[pl.ds(start, inside), :]] * (snaps // LANES), axis=1)
            if inside < chunk:
                own = jnp.concatenate([own, jnp.zeros((chunk - inside, snaps), F32)], axis=0)
            weight = weight - own
        weights[pl.ds(start, chunk), :] = weight.astype(BF16)

    delta = row_offset - col_offset

    def write(first_panel):
        copies = []
        for index, (start, count) in enumerate(size.row_blocks):
            kept = min(count, rows - start)
            at = pl.ds(start, kept)
            every = jnp.concatenate([feats_c0[...], feats_c1[...]], axis=0)
            full = mm(weights[pl.ds(start, count), :], every)[:kept, :cols]
            row_id = lax.broadcasted_iota(jnp.int32, full.shape, 0)
            col_id = lax.broadcasted_iota(jnp.int32, full.shape, 1)
            full = full + jnp.where(col_id - row_id == delta + start, diag_cols[:, pl.ds(0, cols)], 0.0)
            if first_panel:
                used = min(size.packed, cols)
                diag = diag_panel[:, pl.ds(0, used)]
                left = mm_nt(row_block(start, count), panel_w16[...])[:kept, :used]
                inside = min(kept, size.packed - start)
                if inside > 0:
                    own = jnp.concatenate([diag_col[pl.ds(start, inside), :]] * (size.packed // LANES), axis=1)
                    own = (own * schur_q[pl.ds(start, inside), :])[:, :used]
                    if inside < kept:
                        own = jnp.concatenate([own, jnp.zeros((kept - inside, used), F32)], axis=0)
                    left = left + own
                part = full[:, :used] - left * diag
                block_sum[at, pl.ds(0, used)] = part
                if used < cols:
                    block_sum[at, pl.ds(used, cols - used)] = full[:, used:]
            else:
                block_sum[at, :] = full
            copy = pltpu.make_async_copy(block_sum.at[at, :], out.at[at, :], sems.at[index])
            copy.start()
            copies.append(copy)
        for copy in copies:
            copy.wait()

    @pl.when(col_offset == 0)
    def _():
        write(True)

    @pl.when(col_offset != 0)
    def _():
        write(False)


class Sizes:
    def __init__(self, **entries):
        self.__dict__.update(entries)


def eliminate(size, parts, tables, diagonals, known, inverses):
    whole = pl.BlockSpec(memory_space=pltpu.VMEM)
    return pl.pallas_call(
        functools.partial(eliminate_kernel, size),
        in_specs=[whole] * (size.parts + 14),
        out_specs=pl.BlockSpec(memory_space=pl.ANY),
        out_shape=jax.ShapeDtypeStruct((size.rows, size.cols), F32),
        scratch_shapes=[pltpu.VMEM(shape, BF16) for shape in feature_shapes(size)]
        + [
            pltpu.VMEM((size.rows_feats, size.snaps), BF16),
            pltpu.VMEM((size.packed, size.snaps), F32),
            pltpu.VMEM((size.packed, size.snaps), BF16),
            pltpu.VMEM((size.packed, size.packed), F32),
            pltpu.VMEM((size.rows, size.cols), F32),
            pltpu.SemaphoreType.DMA((len(size.row_blocks),)),
        ],
        compiler_params=pltpu.CompilerParams(vmem_limit_bytes=VMEM_LIMIT),
        name="eliminate",
    )(*parts, *tables, *diagonals, *known, *inverses)


def partner(values, axis, distance):
    count = lax.axis_size(axis)
    return lax.ppermute(values, axis, [(i, i ^ distance) for i in range(count)])


def distances(axis):
    count = lax.axis_size(axis)
    assert count & (count - 1) == 0
    return [1 << bit for bit in range(count.bit_length() - 1)]


def row_blocks(rows):
    return [(start, min(176, rows - start)) for start in range(0, rows, 176)]


def per_device(codes, node_scale, basis, regular, feature_order, panel_inverse):
    rank = basis.shape[1]
    count = regular.shape[0]
    rows, cols = count // lax.axis_size("node"), count // lax.axis_size("tm")
    snaps = codes.shape[1] * lax.axis_size("tm")
    panels, width = panel_inverse.shape[:2]
    assert panels == 2 and panels * width <= min(rows, cols) and rank == LANES
    shift = width % LANES
    panel_pad = round_up(width + shift, LANES)
    block = 512
    size = Sizes(
        rank=rank,
        snaps=snaps,
        rows=rows,
        cols=cols,
        block=block,
        parts=lax.axis_size("tm") // 2,
        panel_width=width,
        panel_pad=panel_pad,
        panel_total=panels * width,
        packed=width // LANES * LANES + panel_pad,
        rows_pad=round_up(rows, LANES),
        count=count,
        cols_pad=round_up(cols, LANES),
        chunk=176,
    )
    size.rows_feats = round_up(rows, size.chunk)
    size.row_blocks = row_blocks(size.rows_feats)
    total = project(codes, node_scale, basis)
    gaps = [(0, panel_pad - width)], [(shift, panel_pad - width - shift)]
    inverses = [jnp.pad(panel_inverse[k], gaps[k] * 2) for k in range(2)]

    makers = [lambda: prepare_rows(size, feature_order, regular), lambda: prepare_cols(size, feature_order, regular)]
    makers.append(lambda: inverses)
    made = []
    for distance in distances("node"):
        total = total + partner(total, "node", distance)
        if makers:
            total, ready = lax.optimization_barrier((total, makers.pop(0)()))
            made += ready
    made += [array for maker in makers for array in maker()]
    lead_r, trail_r, one_r, diag_col, diag_panel, lead_c, trail_c, one_c, diag_cols, inverse0, inverse1 = made
    tables = (lead_r, trail_r, one_r, lead_c, trail_c, one_c)

    parts = [total]
    for distance in distances("tm")[:-1]:
        parts = parts + [partner(part, "tm", distance) for part in parts]
    others = [partner(part, "tm", distances("tm")[-1]) for part in parts]
    known = features(size, parts, tables)
    return eliminate(size, others, tables, (diag_col, diag_panel, diag_cols), known, (inverse0, inverse1))


def solution(mesh):
    placed = (P("node", "tm"), P("node"), P("node", None), P(), P(), P())
    return jax.shard_map(per_device, mesh=mesh, in_specs=placed, out_specs=P("node", "tm"), check_vma=False)
```

```python
import functools

import jax
import jax.numpy as jnp
from jax import lax
from jax.experimental import pallas as pl
from jax.experimental.pallas import tpu as pltpu
from jax.sharding import PartitionSpec as P

F32 = jnp.float32
BF16 = jnp.bfloat16
LANES = 128
VMEM_LIMIT = 36 * 1024 * 1024
VMEM_LIMIT_LONG = 54 * 1024 * 1024
SMALL_VMEM = 16 * 1024 * 1024
OWN_AT = 0
FILL = (3, 4, 4, 4)
JOIN = (0, 3, 6, 9)


def round_up(size, multiple):
    return -(-size // multiple) * multiple


def mm(left, right):
    return lax.dot_general(left, right, (((1,), (0,)), ((), ())), preferred_element_type=F32)


def mm_nt(left, right):
    return lax.dot_general(left, right, (((1,), (1,)), ((), ())), preferred_element_type=F32)


def mm_tn(left, right):
    return lax.dot_general(left, right, (((0,), (0,)), ((), ())), preferred_element_type=F32)


def in_hbm(*arrays):
    return [pltpu.with_memory_space_constraint(array, pltpu.HBM) for array in arrays]


def project_kernel(codes_ref, scale_ref, basis_ref, out_ref):
    @pl.when(pl.program_id(0) == 0)
    def _():
        out_ref[...] = jnp.zeros_like(out_ref)

    modes = basis_ref[...].astype(F32).T * scale_ref[...]
    out_ref[...] += mm(modes.astype(BF16), codes_ref[...].astype(F32).astype(BF16))


def project(codes, node_scale, basis):
    nodes, snaps = codes.shape
    rank = basis.shape[1]
    block = nodes // 2 if nodes % 2048 == 0 else nodes
    codes, scale, basis = in_hbm(codes, node_scale.reshape(1, nodes), basis)
    return pl.pallas_call(
        project_kernel,
        grid=(nodes // block,),
        in_specs=[
            pl.BlockSpec((block, snaps), lambda i: (i, 0)),
            pl.BlockSpec((1, block), lambda i: (0, i)),
            pl.BlockSpec((block, rank), lambda i: (i, 0)),
        ],
        out_specs=pl.BlockSpec((rank, snaps), lambda i: (0, 0)),
        out_shape=jax.ShapeDtypeStruct((rank, snaps), F32),
        compiler_params=pltpu.CompilerParams(vmem_limit_bytes=SMALL_VMEM),
        name="project",
    )(codes, scale, basis)


def starts(index, rank):
    return (index * (2 * rank + 3 - index)) // 2


def decode(order, rank):
    modes = lax.broadcasted_iota(jnp.int32, (rank, order.shape[1]), 0)
    first = starts(modes, rank)
    reached = first <= order
    leading = jnp.sum(reached.astype(jnp.int32), axis=0, keepdims=True) - 1
    trailing = order - jnp.max(jnp.where(reached, first - modes, 0), axis=0, keepdims=True)
    return leading, jnp.where(order < 0, -1, trailing)


def column(row):
    return jnp.broadcast_to(row, (LANES, row.shape[1])).T


def take_window(values, offset, length, padded, fill):
    total = round_up(values.shape[1], LANES)
    values = jnp.pad(values, ((0, 0), (0, total - values.shape[1])))
    moved = pltpu.roll(values, lax.rem(total - offset, total), 1)[:, :padded]
    lane = lax.broadcasted_iota(jnp.int32, moved.shape, 1)
    return jnp.where(lane < length, moved, fill)


def prepare_rows_kernel(size, order_ref, regular_ref, lead, trail, one, diag_col, diag_panel):
    count = lead.shape[0]
    offset = lax.axis_index("node") * size.rows
    order = order_ref[...].reshape(1, size.count)
    parts = [take_window(order, offset, size.rows, size.rows_pad, -1)]
    lane = lax.broadcasted_iota(jnp.int32, (1, size.panel_pad), 1)
    for first in (0, size.panel_width):
        tile, shift = first // LANES * LANES, first % LANES
        inside = (lane >= shift) & (lane < shift + size.panel_width)
        parts.append(jnp.where(inside, order[:, tile : tile + size.panel_pad], -1))
    leading, trailing = decode(jnp.concatenate(parts, axis=1), size.rank)
    leading, trailing = column(leading.astype(F32)), column(trailing.astype(F32))
    lane = lax.broadcasted_iota(jnp.int32, (count, LANES), 1).astype(F32)
    lead[...] = (leading == lane).astype(F32).astype(BF16)
    trail[...] = (trailing == lane).astype(F32).astype(BF16)
    one[...] = (trailing == float(size.rank)).astype(F32)
    regular = regular_ref[...].reshape(1, size.count)[:, : size.packed]
    lane = lax.broadcasted_iota(jnp.int32, regular.shape, 1)
    diag = jnp.where(lane < size.panel_total, regular, 0.0)
    diag_panel[...] = diag
    diag_col[...] = column(jnp.where(offset == 0, diag, 0.0))


def prepare_cols_kernel(size, order_ref, regular_ref, lead, trail, one, diag_cols):
    offset = lax.axis_index("tm") * size.cols
    order = take_window(order_ref[...].reshape(1, size.count), offset, size.cols, size.cols_pad, -1)
    diag_cols[...] = take_window(regular_ref[...].reshape(1, size.count), offset, size.cols, size.cols_pad, 0.0)
    leading, trailing = decode(order, size.rank)
    mode = lax.broadcasted_iota(jnp.int32, (size.rank, size.cols_pad), 0)
    lead[...] = (leading == mode).astype(F32).astype(BF16)
    trail[...] = (trailing == mode).astype(F32).astype(BF16)
    one[...] = (trailing == size.rank).astype(F32)


def prepare(kernel, name, size, shapes, feature_order, regular):
    return pl.pallas_call(
        functools.partial(kernel, size),
        in_specs=[pl.BlockSpec(memory_space=pltpu.VMEM)] * 2,
        out_shape=[jax.ShapeDtypeStruct(shape, dtype) for shape, dtype in shapes],
        compiler_params=pltpu.CompilerParams(vmem_limit_bytes=SMALL_VMEM),
        cost_estimate=pl.CostEstimate(flops=3_000_000, bytes_accessed=2_000_000, transcendentals=0),
        name=name,
    )(*in_hbm(feature_order, regular))


def prepare_rows(size, feature_order, regular):
    rows = size.rows_pad + 2 * size.panel_pad
    shapes = [((rows, size.rank), BF16)] * 2 + [((rows, LANES), F32)]
    shapes += [((size.packed, LANES), F32), ((1, size.packed), F32)]
    return prepare(prepare_rows_kernel, "prepare_rows", size, shapes, feature_order, regular)


def prepare_cols(size, feature_order, regular):
    shapes = [((size.rank, size.cols_pad), BF16)] * 2 + [((1, size.cols_pad), F32)] * 2
    return prepare(prepare_cols_kernel, "prepare_cols", size, shapes, feature_order, regular)


def split(values):
    upper = values.astype(BF16)
    return upper, (values - upper.astype(F32)).astype(BF16)


def feature_makers(parts, lead_r, trail_r, one_r, lead_c, trail_c, one_c):
    modes_t = jnp.concatenate([part[...] for part in parts], axis=1)
    snaps = modes_t.shape[1]
    modes2_t = jnp.concatenate(split(modes_t), axis=0)
    modes2 = jnp.concatenate(split(modes_t.T), axis=1)

    def row_features(start, count):
        lead = lead_r[pl.ds(start, count), :]
        trail = trail_r[pl.ds(start, count), :]
        one = one_r[pl.ds(start, count), :]
        former = mm(jnp.concatenate([lead, lead], axis=1), modes2_t)
        latter = mm(jnp.concatenate([trail, trail], axis=1), modes2_t)
        return (former * (latter + jnp.concatenate([one] * (snaps // LANES), axis=1))).astype(BF16)

    def column_features(start, count):
        lead = lead_c[:, pl.ds(start, count)]
        trail = trail_c[:, pl.ds(start, count)]
        former = mm(modes2, jnp.concatenate([lead, lead], axis=0))
        latter = mm(modes2, jnp.concatenate([trail, trail], axis=0)) + one_c[:, pl.ds(start, count)]
        return (former * latter).astype(BF16)

    return row_features, column_features


def features_kernel(size, *refs):
    parts, refs = refs[: size.parts], refs[size.parts :]
    tables, (feats_p, feats_r, feats_c) = refs[:6], refs[6:]
    row_features, column_features = feature_makers(parts, *tables)
    for start in range(0, 2 * size.panel_pad, size.panel_pad):
        feats_p[pl.ds(start, size.panel_pad), :] = row_features(size.rows_pad + start, size.panel_pad)
    for start in range(0, size.rows_feats, size.chunk):
        feats_r[pl.ds(start, size.chunk), :] = row_features(start, size.chunk)
    for start in range(0, size.cols_pad, size.block):
        count = min(size.block, size.cols_pad - start)
        feats_c[:, pl.ds(start, count)] = column_features(start, count)


def feature_shapes(size):
    half = size.snaps // 2
    return [(2 * size.panel_pad, half), (size.rows_feats, half), (half, size.cols_pad)]


def features(size, parts, tables):
    return pl.pallas_call(
        functools.partial(features_kernel, size),
        in_specs=[pl.BlockSpec(memory_space=pltpu.VMEM)] * (size.parts + 6),
        out_shape=[jax.ShapeDtypeStruct(shape, BF16) for shape in feature_shapes(size)],
        compiler_params=pltpu.CompilerParams(vmem_limit_bytes=SMALL_VMEM),
        cost_estimate=pl.CostEstimate(flops=1_000_000_000, bytes_accessed=2_000_000, transcendentals=0),
        name="features",
    )(*parts, *tables)


def eliminate_kernel(size, *refs):
    parts, refs = refs[: size.parts], refs[size.parts :]
    tables, refs = refs[:6], refs[6:]
    diag_col, diag_panel, diag_cols, feats_p0, feats_r0, feats_c0, inverse0, inverse1 = refs[:8]
    out, feats_p1, feats_r1, feats_c1, weights, panel_w, panel_w16, schur_q, block_own, factor, block_sum, sems = refs[8:]
    row_offset = lax.axis_index("node") * size.rows
    col_offset = lax.axis_index("tm") * size.cols
    snaps, block, rows, cols = size.snaps, size.block, size.rows, size.cols
    pad, chunk = size.panel_pad, size.chunk
    inv_snaps = 1.0 / size.snaps
    row_features, column_features = feature_makers(parts, *tables)

    def row_block(start, count):
        at = pl.ds(start, count)
        return jnp.concatenate([feats_r0[at, :], feats_r1[at, :]], axis=1)

    joint = size.panel_width // LANES * LANES
    over = pad - joint

    def pack(upper, lower, axis):
        lead_part = lax.slice_in_dim(upper, 0, joint, axis=axis)
        shared = lax.slice_in_dim(upper, joint, pad, axis=axis) + lax.slice_in_dim(lower, 0, over, axis=axis)
        tail = lax.slice_in_dim(lower, over, pad, axis=axis)
        return jnp.concatenate([lead_part, shared, tail], axis=axis)

    fillers = []

    def fill(count):
        while fillers and count > 0:
            fillers.pop(0)()
            count -= 1

    def make_rows(start):
        feats_r1[pl.ds(start, chunk), :] = row_features(start, chunk)

    def make_columns(start, count):
        feats_c1[:, pl.ds(start, count)] = column_features(start, count)

    panels = []
    for start in range(0, 2 * pad, pad):
        at = pl.ds(start, pad)
        feats_p1[at, :] = row_features(size.rows_pad + start, pad)
        panels.append(jnp.concatenate([feats_p0[at, :], feats_p1[at, :]], axis=1))
    for start in range(0, size.rows_feats, chunk):
        fillers.append(functools.partial(make_rows, start))
    for start in range(0, size.cols_pad, block):
        fillers.append(functools.partial(make_columns, start, min(block, size.cols_pad - start)))
    first, second = panels
    inv0, inv1 = inverse0[...].astype(BF16), inverse1[...].astype(BF16)
    cross = (mm_nt(second, first) * inv_snaps).astype(BF16)
    inner = {}

    def join(turn):
        if turn == 0:
            inner["coupling"] = mm_nt(inv0, cross).astype(BF16)
        elif turn == 1:
            inner["q01"] = -mm(inner["coupling"], inv1)
        elif turn == 2:
            inner["q10"] = -mm_nt(inv1, inner["coupling"])
        else:
            q00 = inverse0[...] - mm_nt(inner["q01"].astype(BF16), inner["coupling"])
            schur_q[...] = pack(pack(q00, inner["q01"], 1), pack(inner["q10"], inverse1[...], 1), 0)

    for turn, place in enumerate(JOIN):
        fillers.insert(place, functools.partial(join, turn))
    scaled0 = mm(inv0, first).astype(BF16)
    fill(FILL[0])
    left1 = (second.astype(F32) - mm(cross, scaled0)).astype(BF16)
    fill(FILL[1])
    scaled1 = mm(inv1, left1)
    fill(FILL[2])
    scaled1_16 = scaled1.astype(BF16)
    spread = mm_tn(jnp.concatenate([first, left1], axis=0), jnp.concatenate([scaled0, scaled1_16], axis=0))
    spread = (spread * inv_snaps).astype(BF16)
    fill(FILL[3])
    fill(len(fillers))
    def make_weights(start, count):
        feats = row_block(start, count)
        weight = (feats.astype(F32) - mm(feats, spread)) * inv_snaps
        inside = min(count, size.packed - start)
        if inside > 0:
            own = panel_w[pl.ds(start, inside), :]
            own = own * jnp.concatenate([diag_col[pl.ds(start, inside), :]] * (snaps // LANES), axis=1)
            if inside < count:
                own = jnp.concatenate([own, jnp.zeros((count - inside, snaps), F32)], axis=0)
            weight = weight - own
        weights[pl.ds(start, count), :] = weight.astype(BF16)

    make_weights(*size.row_blocks[0])
    back = first.astype(F32) - mm_tn(cross, scaled1_16)
    packed = pack(mm(inv0, back.astype(BF16)), scaled1, 0) * inv_snaps
    panel_w[...] = packed
    panel_w16[...] = packed.astype(BF16)
    delta = row_offset - col_offset

    def write(first_panel):
        used = min(size.packed, cols) if first_panel else 0
        edge = round_up(used, LANES)
        here = pl.ds(0, edge)

        def panel_columns():
            return jnp.concatenate([feats_c0[:, here], feats_c1[:, here]], axis=0)

        def make_factor():
            near = panel_columns()
            weighted = (near.astype(F32) - mm(spread, near)) * inv_snaps
            factor[:, here] = (weighted - panel_w[...].T[:, :edge] * diag_panel[:, here]).astype(BF16)

        def make_own():
            own = mm(panel_w16[...], panel_columns()) + schur_q[:, here] * diag_panel[:, here]
            block_own[:, here] = own * jnp.concatenate([diag_col[...]] * (edge // LANES), axis=1)

        copies = []
        for index, (start, count) in enumerate(size.row_blocks):
            if index + 1 < len(size.row_blocks):
                make_weights(*size.row_blocks[index + 1])
            kept = min(count, rows - start)
            at = pl.ds(start, kept)

            def with_diagonal(values, first_col):
                row_id = lax.broadcasted_iota(jnp.int32, values.shape, 0)
                col_id = lax.broadcasted_iota(jnp.int32, values.shape, 1)
                there = col_id - row_id == delta + (start - first_col)
                return values + jnp.where(there, diag_cols[:, pl.ds(first_col, values.shape[1])], 0.0)

            if used < cols:
                rest = pl.ds(edge, size.cols_pad - edge)
                every = jnp.concatenate([feats_c0[:, rest], feats_c1[:, rest]], axis=0)
                right = mm(weights[pl.ds(start, count), :], every)[:kept, : cols - edge]
                block_sum[at, pl.ds(edge, cols - edge)] = with_diagonal(right, edge)
            if first_panel:
                if index == 0:
                    make_factor()
                if index == OWN_AT:
                    make_own()
                left = mm(row_block(start, count), factor[:, here])[:kept, :used]
                inside = min(kept, size.packed - start)
                if inside > 0:
                    mine = block_own[pl.ds(start, inside), pl.ds(0, used)]
                    if inside < kept:
                        mine = jnp.concatenate([mine, jnp.zeros((kept - inside, used), F32)], axis=0)
                    left = left - mine
                block_sum[at, pl.ds(0, used)] = with_diagonal(left, 0)
            copy = pltpu.make_async_copy(block_sum.at[at, :], out.at[at, :], sems.at[index])
            copy.start()
            copies.append(copy)
        for copy in copies:
            copy.wait()

    @pl.when(col_offset == 0)
    def _():
        write(True)

    @pl.when(col_offset != 0)
    def _():
        write(False)


class Sizes:
    def __init__(self, **entries):
        self.__dict__.update(entries)


def eliminate(size, parts, tables, diagonals, known, inverses):
    whole = pl.BlockSpec(memory_space=pltpu.VMEM)
    return pl.pallas_call(
        functools.partial(eliminate_kernel, size),
        in_specs=[whole] * (size.parts + 14),
        out_specs=pl.BlockSpec(memory_space=pl.ANY),
        out_shape=jax.ShapeDtypeStruct((size.rows, size.cols), F32),
        scratch_shapes=[pltpu.VMEM(shape, BF16) for shape in feature_shapes(size)]
        + [
            pltpu.VMEM((size.rows_feats, size.snaps), BF16),
            pltpu.VMEM((size.packed, size.snaps), F32),
            pltpu.VMEM((size.packed, size.snaps), BF16),
            pltpu.VMEM((size.packed, size.packed), F32),
            pltpu.VMEM((size.packed, size.packed), F32),
            pltpu.VMEM((size.snaps, size.packed), BF16),
            pltpu.VMEM((size.rows, size.cols), F32),
            pltpu.SemaphoreType.DMA((len(size.row_blocks),)),
        ],
        compiler_params=pltpu.CompilerParams(vmem_limit_bytes=VMEM_LIMIT if size.snaps <= 512 else VMEM_LIMIT_LONG),
        name="eliminate",
    )(*parts, *tables, *diagonals, *known, *inverses)


def partner(values, axis, distance):
    count = lax.axis_size(axis)
    return lax.ppermute(values, axis, [(i, i ^ distance) for i in range(count)])


def distances(axis):
    count = lax.axis_size(axis)
    assert count & (count - 1) == 0
    return [1 << bit for bit in range(count.bit_length() - 1)]


def row_blocks(rows):
    return [(start, min(176, rows - start)) for start in range(0, rows, 176)][::-1]


def per_device(codes, node_scale, basis, regular, feature_order, panel_inverse):
    rank = basis.shape[1]
    count = regular.shape[0]
    rows, cols = count // lax.axis_size("node"), count // lax.axis_size("tm")
    snaps = codes.shape[1] * lax.axis_size("tm")
    panels, width = panel_inverse.shape[:2]
    assert panels == 2 and panels * width <= min(rows, cols) and rank == LANES
    shift = width % LANES
    panel_pad = round_up(width + shift, LANES)
    block = 512
    size = Sizes(
        rank=rank,
        snaps=snaps,
        rows=rows,
        cols=cols,
        block=block,
        parts=lax.axis_size("tm") // 2,
        panel_width=width,
        panel_pad=panel_pad,
        panel_total=panels * width,
        packed=width // LANES * LANES + panel_pad,
        rows_pad=round_up(rows, LANES),
        count=count,
        cols_pad=round_up(cols, LANES),
        chunk=176,
    )
    size.rows_feats = round_up(rows, size.chunk)
    size.row_blocks = row_blocks(size.rows_feats)
    total = project(codes, node_scale, basis)

    made = []
    for turn, distance in enumerate(distances("node")):
        total = total + partner(total, "node", distance)
        if turn == 0:
            total, ready = lax.optimization_barrier((total, prepare_rows(size, feature_order, regular)))
            made += ready
        elif turn == 1:
            ready = prepare_cols(size, feature_order, regular)
            total, ready, panel_inverse = lax.optimization_barrier((total, ready, panel_inverse))
            made += ready
    lead_r, trail_r, one_r, diag_col, diag_panel, lead_c, trail_c, one_c, diag_cols = made
    tables = (lead_r, trail_r, one_r, lead_c, trail_c, one_c)
    gaps = [(0, panel_pad - width)], [(shift, panel_pad - width - shift)]
    inverses = [jnp.pad(panel_inverse[k], gaps[k] * 2) for k in range(2)]

    *near, last = distances("tm")
    parts, others = [total], [partner(total, "tm", last)]
    for distance in near:
        parts = parts + [partner(part, "tm", distance) for part in parts]
    known = features(size, parts, tables)
    for distance in near:
        others = others + [partner(part, "tm", distance) for part in others]
    return eliminate(size, others, tables, (diag_col, diag_panel, diag_cols), known, inverses)


def solution(mesh):
    placed = (P("node", "tm"), P("node"), P("node", None), P(), P(), P())
    return jax.shard_map(per_device, mesh=mesh, in_specs=placed, out_specs=P("node", "tm"), check_vma=False)
```

```python
import functools

import jax
import jax.numpy as jnp
from jax import lax
from jax.experimental import pallas as pl
from jax.experimental.pallas import tpu as pltpu
from jax.sharding import PartitionSpec as P

F32 = jnp.float32
BF16 = jnp.bfloat16
LANES = 128
VMEM_LIMIT = 36 * 1024 * 1024
VMEM_LIMIT_LONG = 54 * 1024 * 1024
SMALL_VMEM = 16 * 1024 * 1024
OWN_AT = 0
FILL = (3, 4, 4, 4)
JOIN = (0, 3, 6, 9)


def round_up(size, multiple):
    return -(-size // multiple) * multiple


def mm(left, right):
    return lax.dot_general(left, right, (((1,), (0,)), ((), ())), preferred_element_type=F32)


def mm_nt(left, right):
    return lax.dot_general(left, right, (((1,), (1,)), ((), ())), preferred_element_type=F32)


def mm_tn(left, right):
    return lax.dot_general(left, right, (((0,), (0,)), ((), ())), preferred_element_type=F32)


def in_hbm(*arrays):
    return [pltpu.with_memory_space_constraint(array, pltpu.HBM) for array in arrays]


def project_kernel(codes_ref, scale_ref, basis_ref, out_ref):
    @pl.when(pl.program_id(0) == 0)
    def _():
        out_ref[...] = jnp.zeros_like(out_ref)

    modes = basis_ref[...].astype(F32).T * scale_ref[...]
    out_ref[...] += mm(modes.astype(BF16), codes_ref[...].astype(F32).astype(BF16))


def project(codes, node_scale, basis):
    nodes, snaps = codes.shape
    rank = basis.shape[1]
    block = nodes // 2 if nodes % 2048 == 0 else nodes
    codes, scale, basis = in_hbm(codes, node_scale.reshape(1, nodes), basis)
    return pl.pallas_call(
        project_kernel,
        grid=(nodes // block,),
        in_specs=[
            pl.BlockSpec((block, snaps), lambda i: (i, 0)),
            pl.BlockSpec((1, block), lambda i: (0, i)),
            pl.BlockSpec((block, rank), lambda i: (i, 0)),
        ],
        out_specs=pl.BlockSpec((rank, snaps), lambda i: (0, 0)),
        out_shape=jax.ShapeDtypeStruct((rank, snaps), F32),
        compiler_params=pltpu.CompilerParams(vmem_limit_bytes=SMALL_VMEM),
        name="project",
    )(codes, scale, basis)


def starts(index, rank):
    return (index * (2 * rank + 3 - index)) // 2


def decode(order, rank):
    modes = lax.broadcasted_iota(jnp.int32, (rank, order.shape[1]), 0)
    first = starts(modes, rank)
    reached = first <= order
    leading = jnp.sum(reached.astype(jnp.int32), axis=0, keepdims=True) - 1
    trailing = order - jnp.max(jnp.where(reached, first - modes, 0), axis=0, keepdims=True)
    return leading, jnp.where(order < 0, -1, trailing)


def column(row):
    return jnp.broadcast_to(row, (LANES, row.shape[1])).T


def take_window(values, offset, length, padded, fill):
    total = round_up(values.shape[1], LANES)
    values = jnp.pad(values, ((0, 0), (0, total - values.shape[1])))
    moved = pltpu.roll(values, lax.rem(total - offset, total), 1)[:, :padded]
    lane = lax.broadcasted_iota(jnp.int32, moved.shape, 1)
    return jnp.where(lane < length, moved, fill)


def prepare_rows_kernel(size, order_ref, regular_ref, lead, trail, one, diag_col, diag_panel):
    count = lead.shape[0]
    offset = lax.axis_index("node") * size.rows
    order = order_ref[...].reshape(1, size.count)
    parts = [take_window(order, offset, size.rows, size.rows_pad, -1)]
    lane = lax.broadcasted_iota(jnp.int32, (1, size.panel_pad), 1)
    for first in (0, size.panel_width):
        tile, shift = first // LANES * LANES, first % LANES
        inside = (lane >= shift) & (lane < shift + size.panel_width)
        parts.append(jnp.where(inside, order[:, tile : tile + size.panel_pad], -1))
    leading, trailing = decode(jnp.concatenate(parts, axis=1), size.rank)
    leading, trailing = column(leading.astype(F32)), column(trailing.astype(F32))
    lane = lax.broadcasted_iota(jnp.int32, (count, LANES), 1).astype(F32)
    lead[...] = (leading == lane).astype(F32).astype(BF16)
    trail[...] = (trailing == lane).astype(F32).astype(BF16)
    one[...] = (trailing == float(size.rank)).astype(F32)
    regular = regular_ref[...].reshape(1, size.count)[:, : size.packed]
    lane = lax.broadcasted_iota(jnp.int32, regular.shape, 1)
    diag = jnp.where(lane < size.panel_total, regular, 0.0)
    diag_panel[...] = diag
    diag_col[...] = column(jnp.where(offset == 0, diag, 0.0))


def prepare_cols_kernel(size, order_ref, regular_ref, lead, trail, one, diag_cols):
    offset = lax.axis_index("tm") * size.cols
    order = take_window(order_ref[...].reshape(1, size.count), offset, size.cols, size.cols_pad, -1)
    diag_cols[...] = take_window(regular_ref[...].reshape(1, size.count), offset, size.cols, size.cols_pad, 0.0)
    leading, trailing = decode(order, size.rank)
    mode = lax.broadcasted_iota(jnp.int32, (size.rank, size.cols_pad), 0)
    lead[...] = (leading == mode).astype(F32).astype(BF16)
    trail[...] = (trailing == mode).astype(F32).astype(BF16)
    one[...] = (trailing == size.rank).astype(F32)


def prepare(kernel, name, size, shapes, feature_order, regular):
    return pl.pallas_call(
        functools.partial(kernel, size),
        in_specs=[pl.BlockSpec(memory_space=pltpu.VMEM)] * 2,
        out_shape=[jax.ShapeDtypeStruct(shape, dtype) for shape, dtype in shapes],
        compiler_params=pltpu.CompilerParams(vmem_limit_bytes=SMALL_VMEM),
        cost_estimate=pl.CostEstimate(flops=3_000_000, bytes_accessed=2_000_000, transcendentals=0),
        name=name,
    )(*in_hbm(feature_order, regular))


def prepare_rows(size, feature_order, regular):
    rows = size.rows_pad + 2 * size.panel_pad
    shapes = [((rows, size.rank), BF16)] * 2 + [((rows, LANES), F32)]
    shapes += [((size.packed, LANES), F32), ((1, size.packed), F32)]
    return prepare(prepare_rows_kernel, "prepare_rows", size, shapes, feature_order, regular)


def prepare_cols(size, feature_order, regular):
    shapes = [((size.rank, size.cols_pad), BF16)] * 2 + [((1, size.cols_pad), F32)] * 2
    return prepare(prepare_cols_kernel, "prepare_cols", size, shapes, feature_order, regular)


def split(values):
    upper = values.astype(BF16)
    return upper, (values - upper.astype(F32)).astype(BF16)


def feature_makers(parts, lead_r, trail_r, one_r, lead_c, trail_c, one_c):
    modes_t = jnp.concatenate([part[...] for part in parts], axis=1)
    snaps = modes_t.shape[1]
    modes2_t = jnp.concatenate(split(modes_t), axis=0)
    modes2 = jnp.concatenate(split(modes_t.T), axis=1)

    def row_features(start, count):
        lead = lead_r[pl.ds(start, count), :]
        trail = trail_r[pl.ds(start, count), :]
        one = one_r[pl.ds(start, count), :]
        former = mm(jnp.concatenate([lead, lead], axis=1), modes2_t)
        latter = mm(jnp.concatenate([trail, trail], axis=1), modes2_t)
        return (former * (latter + jnp.concatenate([one] * (snaps // LANES), axis=1))).astype(BF16)

    def column_features(start, count):
        lead = lead_c[:, pl.ds(start, count)]
        trail = trail_c[:, pl.ds(start, count)]
        former = mm(modes2, jnp.concatenate([lead, lead], axis=0))
        latter = mm(modes2, jnp.concatenate([trail, trail], axis=0)) + one_c[:, pl.ds(start, count)]
        return (former * latter).astype(BF16)

    return row_features, column_features


def features_kernel(size, count, *refs):
    parts, refs = refs[:count], refs[count:]
    tables, (feats_p, feats_r, feats_c) = refs[:6], refs[6:]
    row_features, column_features = feature_makers(parts, *tables)
    for start in range(0, 2 * size.panel_pad, size.panel_pad):
        feats_p[pl.ds(start, size.panel_pad), :] = row_features(size.rows_pad + start, size.panel_pad)
    for start in range(0, size.rows_feats, size.chunk):
        feats_r[pl.ds(start, size.chunk), :] = row_features(start, size.chunk)
    for start in range(0, size.cols_pad, size.block):
        width = min(size.block, size.cols_pad - start)
        feats_c[:, pl.ds(start, width)] = column_features(start, width)


def feature_shapes(size, parts):
    snaps = sum(part.shape[1] for part in parts)
    return [(2 * size.panel_pad, snaps), (size.rows_feats, snaps), (snaps, size.cols_pad)]


def features(size, parts, tables):
    return pl.pallas_call(
        functools.partial(features_kernel, size, len(parts)),
        in_specs=[pl.BlockSpec(memory_space=pltpu.VMEM)] * (len(parts) + 6),
        out_shape=[jax.ShapeDtypeStruct(shape, BF16) for shape in feature_shapes(size, parts)],
        compiler_params=pltpu.CompilerParams(vmem_limit_bytes=SMALL_VMEM),
        cost_estimate=pl.CostEstimate(flops=500_000_000 * len(parts), bytes_accessed=2_000_000, transcendentals=0),
        name="features",
    )(*parts, *tables)


def eliminate_kernel(size, count, *refs):
    parts, refs = refs[:count], refs[count:]
    tables, refs = refs[:6], refs[6:]
    (diag_col, diag_panel, diag_cols), known, (inverse0, inverse1) = refs[:3], refs[3:9], refs[9:11]
    out, feats_p, feats_r, feats_c, weights, panel_w, panel_w16, schur_q, block_own, factor, block_sum, sems = refs[11:]
    all_p, all_r, all_c = (*known[0::3], feats_p), (*known[1::3], feats_r), (*known[2::3], feats_c)
    row_offset = lax.axis_index("node") * size.rows
    col_offset = lax.axis_index("tm") * size.cols
    snaps, block, rows, cols = size.snaps, size.block, size.rows, size.cols
    pad, chunk = size.panel_pad, size.chunk
    inv_snaps = 1.0 / size.snaps
    row_features, column_features = feature_makers(parts, *tables)

    def row_block(start, count):
        return jnp.concatenate([feats[pl.ds(start, count), :] for feats in all_r], axis=1)

    def column_block(start, count):
        return jnp.concatenate([feats[:, pl.ds(start, count)] for feats in all_c], axis=0)

    joint = size.panel_width // LANES * LANES
    over = pad - joint

    def pack(upper, lower, axis):
        lead_part = lax.slice_in_dim(upper, 0, joint, axis=axis)
        shared = lax.slice_in_dim(upper, joint, pad, axis=axis) + lax.slice_in_dim(lower, 0, over, axis=axis)
        tail = lax.slice_in_dim(lower, over, pad, axis=axis)
        return jnp.concatenate([lead_part, shared, tail], axis=axis)

    fillers = []

    def fill(count):
        while fillers and count > 0:
            fillers.pop(0)()
            count -= 1

    def make_rows(start):
        feats_r[pl.ds(start, chunk), :] = row_features(start, chunk)

    def make_columns(start, count):
        feats_c[:, pl.ds(start, count)] = column_features(start, count)

    panels = []
    for start in range(0, 2 * pad, pad):
        feats_p[pl.ds(start, pad), :] = row_features(size.rows_pad + start, pad)
        panels.append(jnp.concatenate([feats[pl.ds(start, pad), :] for feats in all_p], axis=1))
    for start in range(0, size.rows_feats, chunk):
        fillers.append(functools.partial(make_rows, start))
    for start in range(0, size.cols_pad, block):
        fillers.append(functools.partial(make_columns, start, min(block, size.cols_pad - start)))
    first, second = panels
    inv0, inv1 = inverse0[...].astype(BF16), inverse1[...].astype(BF16)
    cross = (mm_nt(second, first) * inv_snaps).astype(BF16)
    inner = {}

    def join(turn):
        if turn == 0:
            inner["coupling"] = mm_nt(inv0, cross).astype(BF16)
        elif turn == 1:
            inner["q01"] = -mm(inner["coupling"], inv1)
        elif turn == 2:
            inner["q10"] = -mm_nt(inv1, inner["coupling"])
        else:
            q00 = inverse0[...] - mm_nt(inner["q01"].astype(BF16), inner["coupling"])
            schur_q[...] = pack(pack(q00, inner["q01"], 1), pack(inner["q10"], inverse1[...], 1), 0)

    for turn, place in enumerate(JOIN):
        fillers.insert(place, functools.partial(join, turn))
    scaled0 = mm(inv0, first).astype(BF16)
    fill(FILL[0])
    left1 = (second.astype(F32) - mm(cross, scaled0)).astype(BF16)
    fill(FILL[1])
    scaled1 = mm(inv1, left1)
    fill(FILL[2])
    scaled1_16 = scaled1.astype(BF16)
    spread = mm_tn(jnp.concatenate([first, left1], axis=0), jnp.concatenate([scaled0, scaled1_16], axis=0))
    spread = (spread * inv_snaps).astype(BF16)
    fill(FILL[3])
    fill(len(fillers))
    def make_weights(start, count):
        feats = row_block(start, count)
        weight = (feats.astype(F32) - mm(feats, spread)) * inv_snaps
        inside = min(count, size.packed - start)
        if inside > 0:
            own = panel_w[pl.ds(start, inside), :]
            own = own * jnp.concatenate([diag_col[pl.ds(start, inside), :]] * (snaps // LANES), axis=1)
            if inside < count:
                own = jnp.concatenate([own, jnp.zeros((count - inside, snaps), F32)], axis=0)
            weight = weight - own
        weights[pl.ds(start, count), :] = weight.astype(BF16)

    make_weights(*size.row_blocks[0])
    back = first.astype(F32) - mm_tn(cross, scaled1_16)
    packed = pack(mm(inv0, back.astype(BF16)), scaled1, 0) * inv_snaps
    panel_w[...] = packed
    panel_w16[...] = packed.astype(BF16)
    delta = row_offset - col_offset

    def write(first_panel):
        used = min(size.packed, cols) if first_panel else 0
        edge = round_up(used, LANES)
        here = pl.ds(0, edge)

        def panel_columns():
            return column_block(0, edge)

        def make_factor():
            near = panel_columns()
            weighted = (near.astype(F32) - mm(spread, near)) * inv_snaps
            factor[:, here] = (weighted - panel_w[...].T[:, :edge] * diag_panel[:, here]).astype(BF16)

        def make_own():
            own = mm(panel_w16[...], panel_columns()) + schur_q[:, here] * diag_panel[:, here]
            block_own[:, here] = own * jnp.concatenate([diag_col[...]] * (edge // LANES), axis=1)

        copies = []
        for index, (start, count) in enumerate(size.row_blocks):
            if index + 1 < len(size.row_blocks):
                make_weights(*size.row_blocks[index + 1])
            kept = min(count, rows - start)
            at = pl.ds(start, kept)

            def with_diagonal(values, first_col):
                row_id = lax.broadcasted_iota(jnp.int32, values.shape, 0)
                col_id = lax.broadcasted_iota(jnp.int32, values.shape, 1)
                there = col_id - row_id == delta + (start - first_col)
                return values + jnp.where(there, diag_cols[:, pl.ds(first_col, values.shape[1])], 0.0)

            if used < cols:
                every = column_block(edge, size.cols_pad - edge)
                right = mm(weights[pl.ds(start, count), :], every)[:kept, : cols - edge]
                block_sum[at, pl.ds(edge, cols - edge)] = with_diagonal(right, edge)
            if first_panel:
                if index == 0:
                    make_factor()
                if index == OWN_AT:
                    make_own()
                left = mm(row_block(start, count), factor[:, here])[:kept, :used]
                inside = min(kept, size.packed - start)
                if inside > 0:
                    mine = block_own[pl.ds(start, inside), pl.ds(0, used)]
                    if inside < kept:
                        mine = jnp.concatenate([mine, jnp.zeros((kept - inside, used), F32)], axis=0)
                    left = left - mine
                block_sum[at, pl.ds(0, used)] = with_diagonal(left, 0)
            copy = pltpu.make_async_copy(block_sum.at[at, :], out.at[at, :], sems.at[index])
            copy.start()
            copies.append(copy)
        for copy in copies:
            copy.wait()

    @pl.when(col_offset == 0)
    def _():
        write(True)

    @pl.when(col_offset != 0)
    def _():
        write(False)


class Sizes:
    def __init__(self, **entries):
        self.__dict__.update(entries)


def eliminate(size, parts, tables, diagonals, known, inverses):
    whole = pl.BlockSpec(memory_space=pltpu.VMEM)
    return pl.pallas_call(
        functools.partial(eliminate_kernel, size, len(parts)),
        in_specs=[whole] * (len(parts) + 17),
        out_specs=pl.BlockSpec(memory_space=pl.ANY),
        out_shape=jax.ShapeDtypeStruct((size.rows, size.cols), F32),
        scratch_shapes=[pltpu.VMEM(shape, BF16) for shape in feature_shapes(size, parts)]
        + [
            pltpu.VMEM((size.rows_feats, size.snaps), BF16),
            pltpu.VMEM((size.packed, size.snaps), F32),
            pltpu.VMEM((size.packed, size.snaps), BF16),
            pltpu.VMEM((size.packed, size.packed), F32),
            pltpu.VMEM((size.packed, size.packed), F32),
            pltpu.VMEM((size.snaps, size.packed), BF16),
            pltpu.VMEM((size.rows, size.cols), F32),
            pltpu.SemaphoreType.DMA((len(size.row_blocks),)),
        ],
        compiler_params=pltpu.CompilerParams(vmem_limit_bytes=VMEM_LIMIT if size.snaps <= 512 else VMEM_LIMIT_LONG),
        name="eliminate",
    )(*parts, *tables, *diagonals, *known, *inverses)


def partner(values, axis, distance):
    count = lax.axis_size(axis)
    return lax.ppermute(values, axis, [(i, i ^ distance) for i in range(count)])


def distances(axis):
    count = lax.axis_size(axis)
    assert count & (count - 1) == 0
    return [1 << bit for bit in range(count.bit_length() - 1)]


def row_blocks(rows):
    return [(start, min(176, rows - start)) for start in range(0, rows, 176)][::-1]


def per_device(codes, node_scale, basis, regular, feature_order, panel_inverse):
    rank = basis.shape[1]
    count = regular.shape[0]
    rows, cols = count // lax.axis_size("node"), count // lax.axis_size("tm")
    snaps = codes.shape[1] * lax.axis_size("tm")
    panels, width = panel_inverse.shape[:2]
    assert panels == 2 and panels * width <= min(rows, cols) and rank == LANES
    shift = width % LANES
    panel_pad = round_up(width + shift, LANES)
    block = 512
    size = Sizes(
        rank=rank,
        snaps=snaps,
        rows=rows,
        cols=cols,
        block=block,
        panel_width=width,
        panel_pad=panel_pad,
        panel_total=panels * width,
        packed=width // LANES * LANES + panel_pad,
        rows_pad=round_up(rows, LANES),
        count=count,
        cols_pad=round_up(cols, LANES),
        chunk=176,
    )
    size.rows_feats = round_up(rows, size.chunk)
    size.row_blocks = row_blocks(size.rows_feats)
    total = project(codes, node_scale, basis)

    gaps = [(0, panel_pad - width)], [(shift, panel_pad - width - shift)]

    made = []
    for turn, distance in enumerate(distances("node")):
        total = total + partner(total, "node", distance)
        if turn == 0:
            total, ready = lax.optimization_barrier((total, prepare_rows(size, feature_order, regular)))
            made += ready
        elif turn == 1:
            ready = prepare_cols(size, feature_order, regular)
            total, ready, panel_inverse = lax.optimization_barrier((total, ready, panel_inverse))
            made += ready
            inverses = [jnp.pad(panel_inverse[k], gaps[k] * 2) for k in range(2)]
        elif turn == 2:
            total, inverses = lax.optimization_barrier((total, inverses))
    lead_r, trail_r, one_r, diag_col, diag_panel, lead_c, trail_c, one_c, diag_cols = made
    tables = (lead_r, trail_r, one_r, lead_c, trail_c, one_c)
    *near, last = distances("tm")
    parts, others = [total], [partner(total, "tm", last)]
    for distance in near:
        parts = parts + [partner(part, "tm", distance) for part in parts]
    known = features(size, parts, tables)
    others, known = lax.optimization_barrier((others, known))
    for distance in near[:-1]:
        others = others + [partner(part, "tm", distance) for part in others]
    rest = [partner(part, "tm", near[-1]) for part in others]
    known = [*known, *features(size, others, tables)]
    return eliminate(size, rest, tables, (diag_col, diag_panel, diag_cols), known, inverses)


def solution(mesh):
    placed = (P("node", "tm"), P("node"), P("node", None), P(), P(), P())
    return jax.shard_map(per_device, mesh=mesh, in_specs=placed, out_specs=P("node", "tm"), check_vma=False)
```

```python
import functools

import jax
import jax.numpy as jnp
from jax import lax
from jax.experimental import pallas as pl
from jax.experimental.pallas import tpu as pltpu
from jax.sharding import PartitionSpec as P

F32 = jnp.float32
BF16 = jnp.bfloat16
LANES = 128
VMEM_LIMIT = 36 * 1024 * 1024
VMEM_LIMIT_LONG = 54 * 1024 * 1024
SMALL_VMEM = 16 * 1024 * 1024
FILL = (3, 4, 4, 4)
JOIN = (0, 3, 6, 9)


def round_up(size, multiple):
    return -(-size // multiple) * multiple


def mm(left, right):
    return lax.dot_general(left, right, (((1,), (0,)), ((), ())), preferred_element_type=F32)


def mm_nt(left, right):
    return lax.dot_general(left, right, (((1,), (1,)), ((), ())), preferred_element_type=F32)


def mm_tn(left, right):
    return lax.dot_general(left, right, (((0,), (0,)), ((), ())), preferred_element_type=F32)


def in_hbm(*arrays):
    return [pltpu.with_memory_space_constraint(array, pltpu.HBM) for array in arrays]


def project_kernel(codes_ref, scale_ref, basis_ref, out_ref):
    @pl.when(pl.program_id(0) == 0)
    def _():
        out_ref[...] = jnp.zeros_like(out_ref)

    modes = basis_ref[...].astype(F32).T * scale_ref[...]
    out_ref[...] += mm(modes.astype(BF16), codes_ref[...].astype(F32).astype(BF16))


def project(codes, node_scale, basis):
    nodes, snaps = codes.shape
    rank = basis.shape[1]
    block = nodes // 2 if nodes % 2048 == 0 else nodes
    codes, scale, basis = in_hbm(codes, node_scale.reshape(1, nodes), basis)
    return pl.pallas_call(
        project_kernel,
        grid=(nodes // block,),
        in_specs=[
            pl.BlockSpec((block, snaps), lambda i: (i, 0)),
            pl.BlockSpec((1, block), lambda i: (0, i)),
            pl.BlockSpec((block, rank), lambda i: (i, 0)),
        ],
        out_specs=pl.BlockSpec((rank, snaps), lambda i: (0, 0)),
        out_shape=jax.ShapeDtypeStruct((rank, snaps), F32),
        compiler_params=pltpu.CompilerParams(vmem_limit_bytes=SMALL_VMEM),
        name="project",
    )(codes, scale, basis)


def starts(index, rank):
    return (index * (2 * rank + 3 - index)) // 2


def decode(order, rank):
    modes = lax.broadcasted_iota(jnp.int32, (rank, order.shape[1]), 0)
    first = starts(modes, rank)
    reached = first <= order
    leading = jnp.sum(reached.astype(jnp.int32), axis=0, keepdims=True) - 1
    trailing = order - jnp.max(jnp.where(reached, first - modes, 0), axis=0, keepdims=True)
    return leading, jnp.where(order < 0, -1, trailing)


def column(row):
    return jnp.broadcast_to(row, (LANES, row.shape[1])).T


def take_window(values, offset, length, padded, fill):
    total = round_up(values.shape[1], LANES)
    values = jnp.pad(values, ((0, 0), (0, total - values.shape[1])))
    moved = pltpu.roll(values, lax.rem(total - offset, total), 1)[:, :padded]
    lane = lax.broadcasted_iota(jnp.int32, moved.shape, 1)
    return jnp.where(lane < length, moved, fill)


def prepare_rows_kernel(size, order_ref, regular_ref, lead, trail, one, diag_col, diag_panel):
    count = lead.shape[0]
    offset = lax.axis_index("node") * size.rows
    order = order_ref[...].reshape(1, size.count)
    parts = [take_window(order, offset, size.rows, size.rows_pad, -1)]
    lane = lax.broadcasted_iota(jnp.int32, (1, size.panel_pad), 1)
    for first in (0, size.panel_width):
        tile, shift = first // LANES * LANES, first % LANES
        inside = (lane >= shift) & (lane < shift + size.panel_width)
        parts.append(jnp.where(inside, order[:, tile : tile + size.panel_pad], -1))
    leading, trailing = decode(jnp.concatenate(parts, axis=1), size.rank)
    leading, trailing = column(leading.astype(F32)), column(trailing.astype(F32))
    lane = lax.broadcasted_iota(jnp.int32, (count, LANES), 1).astype(F32)
    lead[...] = (leading == lane).astype(F32).astype(BF16)
    trail[...] = (trailing == lane).astype(F32).astype(BF16)
    one[...] = (trailing == float(size.rank)).astype(F32)
    regular = regular_ref[...].reshape(1, size.count)[:, : size.packed]
    lane = lax.broadcasted_iota(jnp.int32, regular.shape, 1)
    diag = jnp.where(lane < size.panel_total, regular, 0.0)
    diag_panel[...] = diag
    diag_col[...] = column(jnp.where(offset == 0, diag, 0.0))


def prepare_cols_kernel(size, order_ref, regular_ref, lead, trail, one, diag_cols):
    offset = lax.axis_index("tm") * size.cols
    order = take_window(order_ref[...].reshape(1, size.count), offset, size.cols, size.cols_pad, -1)
    diag_cols[...] = take_window(regular_ref[...].reshape(1, size.count), offset, size.cols, size.cols_pad, 0.0)
    leading, trailing = decode(order, size.rank)
    mode = lax.broadcasted_iota(jnp.int32, (size.rank, size.cols_pad), 0)
    lead[...] = (leading == mode).astype(F32).astype(BF16)
    trail[...] = (trailing == mode).astype(F32).astype(BF16)
    one[...] = (trailing == size.rank).astype(F32)


def prepare(kernel, name, size, shapes, feature_order, regular):
    return pl.pallas_call(
        functools.partial(kernel, size),
        in_specs=[pl.BlockSpec(memory_space=pltpu.VMEM)] * 2,
        out_shape=[jax.ShapeDtypeStruct(shape, dtype) for shape, dtype in shapes],
        compiler_params=pltpu.CompilerParams(vmem_limit_bytes=SMALL_VMEM),
        cost_estimate=pl.CostEstimate(flops=3_000_000, bytes_accessed=2_000_000, transcendentals=0),
        name=name,
    )(*in_hbm(feature_order, regular))


def prepare_rows(size, feature_order, regular):
    rows = size.rows_pad + 2 * size.panel_pad
    shapes = [((rows, size.rank), BF16)] * 2 + [((rows, LANES), F32)]
    shapes += [((size.packed, LANES), F32), ((1, size.packed), F32)]
    return prepare(prepare_rows_kernel, "prepare_rows", size, shapes, feature_order, regular)


def prepare_cols(size, feature_order, regular):
    shapes = [((size.rank, size.cols_pad), BF16)] * 2 + [((1, size.cols_pad), F32)] * 2
    return prepare(prepare_cols_kernel, "prepare_cols", size, shapes, feature_order, regular)


def split(values):
    upper = values.astype(BF16)
    return upper, (values - upper.astype(F32)).astype(BF16)


def feature_makers(parts, lead_r, trail_r, one_r, lead_c, trail_c, one_c):
    modes_t = jnp.concatenate([part[...] for part in parts], axis=1)
    snaps = modes_t.shape[1]
    modes2_t = jnp.concatenate(split(modes_t), axis=0)
    modes2 = jnp.concatenate(split(modes_t.T), axis=1)

    def row_features(start, count):
        lead = lead_r[pl.ds(start, count), :]
        trail = trail_r[pl.ds(start, count), :]
        one = one_r[pl.ds(start, count), :]
        former = mm(jnp.concatenate([lead, lead], axis=1), modes2_t)
        latter = mm(jnp.concatenate([trail, trail], axis=1), modes2_t)
        return (former * (latter + jnp.concatenate([one] * (snaps // LANES), axis=1))).astype(BF16)

    def column_features(start, count):
        lead = lead_c[:, pl.ds(start, count)]
        trail = trail_c[:, pl.ds(start, count)]
        former = mm(modes2, jnp.concatenate([lead, lead], axis=0))
        latter = mm(modes2, jnp.concatenate([trail, trail], axis=0)) + one_c[:, pl.ds(start, count)]
        return (former * latter).astype(BF16)

    return row_features, column_features


def features_kernel(size, count, *refs):
    parts, refs = refs[:count], refs[count:]
    tables, (feats_p, feats_r, feats_c) = refs[:6], refs[6:]
    row_features, column_features = feature_makers(parts, *tables)
    for start in range(0, 2 * size.panel_pad, size.panel_pad):
        feats_p[pl.ds(start, size.panel_pad), :] = row_features(size.rows_pad + start, size.panel_pad)
    for start in range(0, size.rows_feats, size.chunk):
        feats_r[pl.ds(start, size.chunk), :] = row_features(start, size.chunk)
    for start in range(0, size.cols_pad, size.block):
        width = min(size.block, size.cols_pad - start)
        feats_c[:, pl.ds(start, width)] = column_features(start, width)


def feature_shapes(size, parts):
    snaps = sum(part.shape[1] for part in parts)
    return [(2 * size.panel_pad, snaps), (size.rows_feats, snaps), (snaps, size.cols_pad)]


def features(size, parts, tables):
    return pl.pallas_call(
        functools.partial(features_kernel, size, len(parts)),
        in_specs=[pl.BlockSpec(memory_space=pltpu.VMEM)] * (len(parts) + 6),
        out_shape=[jax.ShapeDtypeStruct(shape, BF16) for shape in feature_shapes(size, parts)],
        compiler_params=pltpu.CompilerParams(vmem_limit_bytes=SMALL_VMEM),
        cost_estimate=pl.CostEstimate(flops=500_000_000 * len(parts), bytes_accessed=2_000_000, transcendentals=0),
        name="features",
    )(*parts, *tables)


def eliminate_kernel(size, count, *refs):
    parts, refs = refs[:count], refs[count:]
    tables, refs = refs[:6], refs[6:]
    (diag_col, diag_panel, diag_cols), known, (inverse0, inverse1) = refs[:3], refs[3:9], refs[9:11]
    out, feats_p, feats_r, feats_c, weights, panel_w, panel_w16, schur_q, block_own, factor, block_sum, sems = refs[11:]
    all_p, all_r, all_c = (*known[0::3], feats_p), (*known[1::3], feats_r), (*known[2::3], feats_c)
    row_offset = lax.axis_index("node") * size.rows
    col_offset = lax.axis_index("tm") * size.cols
    snaps, block, rows, cols = size.snaps, size.block, size.rows, size.cols
    pad, chunk = size.panel_pad, size.chunk
    inv_snaps = 1.0 / size.snaps
    row_features, column_features = feature_makers(parts, *tables)

    def row_block(start, count):
        return jnp.concatenate([feats[pl.ds(start, count), :] for feats in all_r], axis=1)

    def column_block(start, count):
        return jnp.concatenate([feats[:, pl.ds(start, count)] for feats in all_c], axis=0)

    joint = size.panel_width // LANES * LANES
    over = pad - joint

    def pack(upper, lower, axis):
        lead_part = lax.slice_in_dim(upper, 0, joint, axis=axis)
        shared = lax.slice_in_dim(upper, joint, pad, axis=axis) + lax.slice_in_dim(lower, 0, over, axis=axis)
        tail = lax.slice_in_dim(lower, over, pad, axis=axis)
        return jnp.concatenate([lead_part, shared, tail], axis=axis)

    fillers = []

    def fill(count):
        while fillers and count > 0:
            fillers.pop(0)()
            count -= 1

    def make_rows(start):
        feats_r[pl.ds(start, chunk), :] = row_features(start, chunk)

    def make_columns(start, count):
        feats_c[:, pl.ds(start, count)] = column_features(start, count)

    panels = []
    for start in range(0, 2 * pad, pad):
        feats_p[pl.ds(start, pad), :] = row_features(size.rows_pad + start, pad)
        panels.append(jnp.concatenate([feats[pl.ds(start, pad), :] for feats in all_p], axis=1))
    for start in range(0, size.rows_feats, chunk):
        fillers.append(functools.partial(make_rows, start))
    for start in range(0, size.cols_pad, block):
        fillers.append(functools.partial(make_columns, start, min(block, size.cols_pad - start)))
    first, second = panels
    inv0, inv1 = inverse0[...].astype(BF16), inverse1[...].astype(BF16)
    cross = (mm_nt(second, first) * inv_snaps).astype(BF16)
    inner = {}

    def join(turn):
        if turn == 0:
            inner["coupling"] = mm_nt(inv0, cross).astype(BF16)
        elif turn == 1:
            inner["q01"] = -mm(inner["coupling"], inv1)
        elif turn == 2:
            inner["q10"] = -mm_nt(inv1, inner["coupling"])
        else:
            q00 = inverse0[...] - mm_nt(inner["q01"].astype(BF16), inner["coupling"])
            schur_q[...] = pack(pack(q00, inner["q01"], 1), pack(inner["q10"], inverse1[...], 1), 0)

    for turn, place in enumerate(JOIN):
        fillers.insert(place, functools.partial(join, turn))
    scaled0 = mm(inv0, first).astype(BF16)
    fill(FILL[0])
    left1 = (second.astype(F32) - mm(cross, scaled0)).astype(BF16)
    fill(FILL[1])
    scaled1 = mm(inv1, left1)
    fill(FILL[2])
    scaled1_16 = scaled1.astype(BF16)
    spread = mm_tn(jnp.concatenate([first, left1], axis=0), jnp.concatenate([scaled0, scaled1_16], axis=0))
    spread = (spread * inv_snaps).astype(BF16)
    fill(FILL[3])
    fill(len(fillers))
    def make_weights(start, count):
        feats = row_block(start, count)
        weight = (feats.astype(F32) - mm(feats, spread)) * inv_snaps
        inside = min(count, size.packed - start)
        if inside > 0:
            own = panel_w[pl.ds(start, inside), :]
            own = own * jnp.concatenate([diag_col[pl.ds(start, inside), :]] * (snaps // LANES), axis=1)
            if inside < count:
                own = jnp.concatenate([own, jnp.zeros((count - inside, snaps), F32)], axis=0)
            weight = weight - own
        weights[pl.ds(start, count), :] = weight.astype(BF16)

    make_weights(*size.row_blocks[0])
    back = first.astype(F32) - mm_tn(cross, scaled1_16)
    packed = pack(mm(inv0, back.astype(BF16)), scaled1, 0) * inv_snaps
    panel_w[...] = packed
    panel_w16[...] = packed.astype(BF16)
    panel_cols = min(size.packed, size.cols_pad)
    here = pl.ds(0, panel_cols)
    near = column_block(0, panel_cols)
    own = mm(panel_w16[...], near) + schur_q[:, here] * diag_panel[:, here]
    block_own[:, here] = own * jnp.concatenate([diag_col[...]] * (panel_cols // LANES), axis=1)
    weighted = (near.astype(F32) - mm(spread, near)) * inv_snaps
    factor[:, here] = (weighted - panel_w[...].T[:, :panel_cols] * diag_panel[:, here]).astype(BF16)

    delta = row_offset - col_offset

    def write(first_panel):
        used = min(size.packed, cols) if first_panel else 0
        edge = round_up(used, LANES)
        here = pl.ds(0, edge)
        copies = []
        for index, (start, count) in enumerate(size.row_blocks):
            if index + 1 < len(size.row_blocks):
                make_weights(*size.row_blocks[index + 1])
            kept = min(count, rows - start)
            at = pl.ds(start, kept)

            def with_diagonal(values, first_col):
                row_id = lax.broadcasted_iota(jnp.int32, values.shape, 0)
                col_id = lax.broadcasted_iota(jnp.int32, values.shape, 1)
                there = col_id - row_id == delta + (start - first_col)
                return values + jnp.where(there, diag_cols[:, pl.ds(first_col, values.shape[1])], 0.0)

            if used < cols:
                every = column_block(edge, size.cols_pad - edge)
                right = mm(weights[pl.ds(start, count), :], every)[:kept, : cols - edge]
                block_sum[at, pl.ds(edge, cols - edge)] = with_diagonal(right, edge)
            if first_panel:
                left = mm(row_block(start, count), factor[:, here])[:kept, :used]
                inside = min(kept, size.packed - start)
                if inside > 0:
                    mine = block_own[pl.ds(start, inside), pl.ds(0, used)]
                    if inside < kept:
                        mine = jnp.concatenate([mine, jnp.zeros((kept - inside, used), F32)], axis=0)
                    left = left - mine
                block_sum[at, pl.ds(0, used)] = with_diagonal(left, 0)
            copy = pltpu.make_async_copy(block_sum.at[at, :], out.at[at, :], sems.at[index])
            copy.start()
            copies.append(copy)
        for copy in copies:
            copy.wait()

    @pl.when(col_offset == 0)
    def _():
        write(True)

    @pl.when(col_offset != 0)
    def _():
        write(False)


class Sizes:
    def __init__(self, **entries):
        self.__dict__.update(entries)


def eliminate(size, parts, tables, diagonals, known, inverses):
    whole = pl.BlockSpec(memory_space=pltpu.VMEM)
    return pl.pallas_call(
        functools.partial(eliminate_kernel, size, len(parts)),
        in_specs=[whole] * (len(parts) + 17),
        out_specs=pl.BlockSpec(memory_space=pl.ANY),
        out_shape=jax.ShapeDtypeStruct((size.rows, size.cols), F32),
        scratch_shapes=[pltpu.VMEM(shape, BF16) for shape in feature_shapes(size, parts)]
        + [
            pltpu.VMEM((size.rows_feats, size.snaps), BF16),
            pltpu.VMEM((size.packed, size.snaps), F32),
            pltpu.VMEM((size.packed, size.snaps), BF16),
            pltpu.VMEM((size.packed, size.packed), F32),
            pltpu.VMEM((size.packed, size.packed), F32),
            pltpu.VMEM((size.snaps, size.packed), BF16),
            pltpu.VMEM((size.rows, size.cols), F32),
            pltpu.SemaphoreType.DMA((len(size.row_blocks),)),
        ],
        compiler_params=pltpu.CompilerParams(vmem_limit_bytes=VMEM_LIMIT if size.snaps <= 512 else VMEM_LIMIT_LONG),
        name="eliminate",
    )(*parts, *tables, *diagonals, *known, *inverses)


def partner(values, axis, distance):
    count = lax.axis_size(axis)
    return lax.ppermute(values, axis, [(i, i ^ distance) for i in range(count)])


def distances(axis):
    count = lax.axis_size(axis)
    assert count & (count - 1) == 0
    return [1 << bit for bit in range(count.bit_length() - 1)]


def row_blocks(rows):
    return [(start, min(176, rows - start)) for start in range(0, rows, 176)][::-1]


def per_device(codes, node_scale, basis, regular, feature_order, panel_inverse):
    rank = basis.shape[1]
    count = regular.shape[0]
    rows, cols = count // lax.axis_size("node"), count // lax.axis_size("tm")
    snaps = codes.shape[1] * lax.axis_size("tm")
    panels, width = panel_inverse.shape[:2]
    assert panels == 2 and panels * width <= min(rows, cols) and rank == LANES
    shift = width % LANES
    panel_pad = round_up(width + shift, LANES)
    block = 512
    size = Sizes(
        rank=rank,
        snaps=snaps,
        rows=rows,
        cols=cols,
        block=block,
        panel_width=width,
        panel_pad=panel_pad,
        panel_total=panels * width,
        packed=width // LANES * LANES + panel_pad,
        rows_pad=round_up(rows, LANES),
        count=count,
        cols_pad=round_up(cols, LANES),
        chunk=176,
    )
    size.rows_feats = round_up(rows, size.chunk)
    size.row_blocks = row_blocks(size.rows_feats)
    total = project(codes, node_scale, basis)

    gaps = [(0, panel_pad - width)], [(shift, panel_pad - width - shift)]

    made = []
    for turn, distance in enumerate(distances("node")):
        total = total + partner(total, "node", distance)
        if turn == 0:
            total, ready = lax.optimization_barrier((total, prepare_rows(size, feature_order, regular)))
            made += ready
        elif turn == 1:
            ready = prepare_cols(size, feature_order, regular)
            total, ready, panel_inverse = lax.optimization_barrier((total, ready, panel_inverse))
            made += ready
            inverses = [jnp.pad(panel_inverse[k], gaps[k] * 2) for k in range(2)]
        elif turn == 2:
            total, inverses = lax.optimization_barrier((total, inverses))
    lead_r, trail_r, one_r, diag_col, diag_panel, lead_c, trail_c, one_c, diag_cols = made
    tables = (lead_r, trail_r, one_r, lead_c, trail_c, one_c)
    *near, last = distances("tm")
    parts, others = [total], [partner(total, "tm", last)]
    for distance in near:
        parts = parts + [partner(part, "tm", distance) for part in parts]
    known = features(size, parts, tables)
    others, known = lax.optimization_barrier((others, known))
    for distance in near[:-1]:
        others = others + [partner(part, "tm", distance) for part in others]
    rest = [partner(part, "tm", near[-1]) for part in others]
    known = [*known, *features(size, others, tables)]
    return eliminate(size, rest, tables, (diag_col, diag_panel, diag_cols), known, inverses)


def solution(mesh):
    placed = (P("node", "tm"), P("node"), P("node", None), P(), P(), P())
    return jax.shard_map(per_device, mesh=mesh, in_specs=placed, out_specs=P("node", "tm"), check_vma=False)
```

```python
import functools

import jax
import jax.numpy as jnp
from jax import lax
from jax.experimental import pallas as pl
from jax.experimental.pallas import tpu as pltpu
from jax.sharding import PartitionSpec as P

F32 = jnp.float32
BF16 = jnp.bfloat16
LANES = 128
VMEM_LIMIT = 36 * 1024 * 1024
VMEM_LIMIT_LONG = 54 * 1024 * 1024
SMALL_VMEM = 16 * 1024 * 1024
FILL = (3, 4, 4, 4)
JOIN = (0, 3, 6, 9)


def round_up(size, multiple):
    return -(-size // multiple) * multiple


def mm(left, right):
    return lax.dot_general(left, right, (((1,), (0,)), ((), ())), preferred_element_type=F32)


def mm_nt(left, right):
    return lax.dot_general(left, right, (((1,), (1,)), ((), ())), preferred_element_type=F32)


def mm_tn(left, right):
    return lax.dot_general(left, right, (((0,), (0,)), ((), ())), preferred_element_type=F32)


def in_hbm(*arrays):
    return [pltpu.with_memory_space_constraint(array, pltpu.HBM) for array in arrays]


def project_kernel(codes_ref, scale_ref, basis_ref, out_ref):
    @pl.when(pl.program_id(0) == 0)
    def _():
        out_ref[...] = jnp.zeros_like(out_ref)

    modes = basis_ref[...].T.astype(F32) * scale_ref[...]
    out_ref[...] += mm(modes.astype(BF16), codes_ref[...].astype(F32).astype(BF16))


def project(codes, node_scale, basis):
    nodes, snaps = codes.shape
    rank = basis.shape[1]
    block = nodes // 2 if nodes % 2048 == 0 else nodes
    codes, scale, basis = in_hbm(codes, node_scale.reshape(1, nodes), basis)
    return pl.pallas_call(
        project_kernel,
        grid=(nodes // block,),
        in_specs=[
            pl.BlockSpec((block, snaps), lambda i: (i, 0)),
            pl.BlockSpec((1, block), lambda i: (0, i)),
            pl.BlockSpec((block, rank), lambda i: (i, 0)),
        ],
        out_specs=pl.BlockSpec((rank, snaps), lambda i: (0, 0)),
        out_shape=jax.ShapeDtypeStruct((rank, snaps), F32),
        compiler_params=pltpu.CompilerParams(vmem_limit_bytes=SMALL_VMEM),
        name="project",
    )(codes, scale, basis)


def starts(index, rank):
    return (index * (2 * rank + 3 - index)) // 2


def decode(order, rank):
    modes = lax.broadcasted_iota(jnp.int32, (rank, order.shape[1]), 0)
    first = starts(modes, rank)
    reached = first <= order
    leading = jnp.sum(reached.astype(jnp.int32), axis=0, keepdims=True) - 1
    trailing = order - jnp.max(jnp.where(reached, first - modes, 0), axis=0, keepdims=True)
    return leading, jnp.where(order < 0, -1, trailing)


def column(row):
    return jnp.broadcast_to(row, (LANES, row.shape[1])).T


def take_window(values, offset, length, padded, fill):
    total = round_up(values.shape[1], LANES)
    values = jnp.pad(values, ((0, 0), (0, total - values.shape[1])))
    moved = pltpu.roll(values, lax.rem(total - offset, total), 1)[:, :padded]
    lane = lax.broadcasted_iota(jnp.int32, moved.shape, 1)
    return jnp.where(lane < length, moved, fill)


def prepare_rows_kernel(size, order_ref, regular_ref, lead, trail, one, diag_col, diag_panel):
    count = lead.shape[0]
    offset = lax.axis_index("node") * size.rows
    order = order_ref[...].reshape(1, size.count)
    parts = [take_window(order, offset, size.rows, size.rows_pad, -1)]
    lane = lax.broadcasted_iota(jnp.int32, (1, size.panel_pad), 1)
    for first in (0, size.panel_width):
        tile, shift = first // LANES * LANES, first % LANES
        inside = (lane >= shift) & (lane < shift + size.panel_width)
        parts.append(jnp.where(inside, order[:, tile : tile + size.panel_pad], -1))
    leading, trailing = decode(jnp.concatenate(parts, axis=1), size.rank)
    leading, trailing = column(leading.astype(F32)), column(trailing.astype(F32))
    lane = lax.broadcasted_iota(jnp.int32, (count, LANES), 1).astype(F32)
    lead[...] = (leading == lane).astype(F32).astype(BF16)
    trail[...] = (trailing == lane).astype(F32).astype(BF16)
    one[...] = (trailing == float(size.rank)).astype(F32)
    regular = regular_ref[...].reshape(1, size.count)[:, : size.packed]
    lane = lax.broadcasted_iota(jnp.int32, regular.shape, 1)
    diag = jnp.where(lane < size.panel_total, regular, 0.0)
    diag_panel[...] = diag
    diag_col[...] = column(jnp.where(offset == 0, diag, 0.0))


def prepare_cols_kernel(size, order_ref, regular_ref, lead, trail, one, diag_cols):
    offset = lax.axis_index("tm") * size.cols
    order = take_window(order_ref[...].reshape(1, size.count), offset, size.cols, size.cols_pad, -1)
    diag_cols[...] = take_window(regular_ref[...].reshape(1, size.count), offset, size.cols, size.cols_pad, 0.0)
    leading, trailing = decode(order, size.rank)
    mode = lax.broadcasted_iota(jnp.int32, (size.rank, size.cols_pad), 0)
    lead[...] = (leading == mode).astype(F32).astype(BF16)
    trail[...] = (trailing == mode).astype(F32).astype(BF16)
    one[...] = (trailing == size.rank).astype(F32)


def prepare(kernel, name, size, shapes, feature_order, regular):
    return pl.pallas_call(
        functools.partial(kernel, size),
        in_specs=[pl.BlockSpec(memory_space=pltpu.VMEM)] * 2,
        out_shape=[jax.ShapeDtypeStruct(shape, dtype) for shape, dtype in shapes],
        compiler_params=pltpu.CompilerParams(vmem_limit_bytes=SMALL_VMEM),
        cost_estimate=pl.CostEstimate(flops=3_000_000, bytes_accessed=2_000_000, transcendentals=0),
        name=name,
    )(*in_hbm(feature_order, regular))


def prepare_rows(size, feature_order, regular):
    rows = size.rows_pad + 2 * size.panel_pad
    shapes = [((rows, size.rank), BF16)] * 2 + [((rows, LANES), F32)]
    shapes += [((size.packed, LANES), F32), ((1, size.packed), F32)]
    return prepare(prepare_rows_kernel, "prepare_rows", size, shapes, feature_order, regular)


def prepare_cols(size, feature_order, regular):
    shapes = [((size.rank, size.cols_pad), BF16)] * 2 + [((1, size.cols_pad), F32)] * 2
    return prepare(prepare_cols_kernel, "prepare_cols", size, shapes, feature_order, regular)


def split(values):
    upper = values.astype(BF16)
    return upper, (values - upper.astype(F32)).astype(BF16)


def feature_makers(parts, lead_r, trail_r, one_r, lead_c, trail_c, one_c):
    modes_t = jnp.concatenate([part[...] for part in parts], axis=1)
    snaps = modes_t.shape[1]
    modes2_t = jnp.concatenate(split(modes_t), axis=0)
    modes2 = jnp.concatenate(split(modes_t.T), axis=1)

    def row_features(start, count):
        lead = lead_r[pl.ds(start, count), :]
        trail = trail_r[pl.ds(start, count), :]
        one = one_r[pl.ds(start, count), :]
        former = mm(jnp.concatenate([lead, lead], axis=1), modes2_t)
        latter = mm(jnp.concatenate([trail, trail], axis=1), modes2_t)
        return (former * (latter + jnp.concatenate([one] * (snaps // LANES), axis=1))).astype(BF16)

    def column_features(start, count):
        lead = lead_c[:, pl.ds(start, count)]
        trail = trail_c[:, pl.ds(start, count)]
        former = mm(modes2, jnp.concatenate([lead, lead], axis=0))
        latter = mm(modes2, jnp.concatenate([trail, trail], axis=0)) + one_c[:, pl.ds(start, count)]
        return (former * latter).astype(BF16)

    return row_features, column_features


def features_kernel(size, count, *refs):
    parts, refs = refs[:count], refs[count:]
    tables, (feats_p, feats_r, feats_c) = refs[:6], refs[6:]
    row_features, column_features = feature_makers(parts, *tables)
    for start in range(0, 2 * size.panel_pad, size.panel_pad):
        feats_p[pl.ds(start, size.panel_pad), :] = row_features(size.rows_pad + start, size.panel_pad)
    for start in range(0, size.rows_feats, size.chunk):
        feats_r[pl.ds(start, size.chunk), :] = row_features(start, size.chunk)
    for start in range(0, size.cols_pad, size.block):
        width = min(size.block, size.cols_pad - start)
        feats_c[:, pl.ds(start, width)] = column_features(start, width)


def feature_shapes(size, parts):
    snaps = sum(part.shape[1] for part in parts)
    return [(2 * size.panel_pad, snaps), (size.rows_feats, snaps), (snaps, size.cols_pad)]


def features(size, parts, tables):
    return pl.pallas_call(
        functools.partial(features_kernel, size, len(parts)),
        in_specs=[pl.BlockSpec(memory_space=pltpu.VMEM)] * (len(parts) + 6),
        out_shape=[jax.ShapeDtypeStruct(shape, BF16) for shape in feature_shapes(size, parts)],
        compiler_params=pltpu.CompilerParams(vmem_limit_bytes=SMALL_VMEM),
        cost_estimate=pl.CostEstimate(flops=500_000_000 * len(parts), bytes_accessed=2_000_000, transcendentals=0),
        name="features",
    )(*parts, *tables)


def eliminate_kernel(size, count, *refs):
    parts, refs = refs[:count], refs[count:]
    tables, refs = refs[:6], refs[6:]
    (diag_col, diag_panel, diag_cols), known, (inverse0, inverse1) = refs[:3], refs[3:9], refs[9:11]
    out, feats_p, feats_r, feats_c, weights, panel_w, panel_w16, schur_q, block_own, factor, block_sum, sems = refs[11:]
    all_p, all_r, all_c = (*known[0::3], feats_p), (*known[1::3], feats_r), (*known[2::3], feats_c)
    row_offset = lax.axis_index("node") * size.rows
    col_offset = lax.axis_index("tm") * size.cols
    snaps, block, rows, cols = size.snaps, size.block, size.rows, size.cols
    pad, chunk = size.panel_pad, size.chunk
    inv_snaps = 1.0 / size.snaps
    row_features, column_features = feature_makers(parts, *tables)

    def row_block(start, count):
        return jnp.concatenate([feats[pl.ds(start, count), :] for feats in all_r], axis=1)

    def column_block(start, count):
        return jnp.concatenate([feats[:, pl.ds(start, count)] for feats in all_c], axis=0)

    joint = size.panel_width // LANES * LANES
    over = pad - joint

    def pack(upper, lower, axis):
        lead_part = lax.slice_in_dim(upper, 0, joint, axis=axis)
        shared = lax.slice_in_dim(upper, joint, pad, axis=axis) + lax.slice_in_dim(lower, 0, over, axis=axis)
        tail = lax.slice_in_dim(lower, over, pad, axis=axis)
        return jnp.concatenate([lead_part, shared, tail], axis=axis)

    fillers = []

    def fill(count):
        while fillers and count > 0:
            fillers.pop(0)()
            count -= 1

    def make_rows(start):
        feats_r[pl.ds(start, chunk), :] = row_features(start, chunk)

    def make_columns(start, count):
        feats_c[:, pl.ds(start, count)] = column_features(start, count)

    panels = []
    for start in range(0, 2 * pad, pad):
        feats_p[pl.ds(start, pad), :] = row_features(size.rows_pad + start, pad)
        panels.append(jnp.concatenate([feats[pl.ds(start, pad), :] for feats in all_p], axis=1))
    for start in range(0, size.rows_feats, chunk):
        fillers.append(functools.partial(make_rows, start))
    for start in range(0, size.cols_pad, block):
        fillers.append(functools.partial(make_columns, start, min(block, size.cols_pad - start)))
    first, second = panels
    inv0, inv1 = inverse0[...].astype(BF16), inverse1[...].astype(BF16)
    cross = (mm_nt(second, first) * inv_snaps).astype(BF16)
    inner = {}

    def join(turn):
        if turn == 0:
            inner["coupling"] = mm_nt(inv0, cross).astype(BF16)
        elif turn == 1:
            inner["q01"] = -mm(inner["coupling"], inv1)
        elif turn == 2:
            inner["q10"] = -mm_nt(inv1, inner["coupling"])
        else:
            q00 = inverse0[...] - mm_nt(inner["q01"].astype(BF16), inner["coupling"])
            schur_q[...] = pack(pack(q00, inner["q01"], 1), pack(inner["q10"], inverse1[...], 1), 0)

    for turn, place in enumerate(JOIN):
        fillers.insert(place, functools.partial(join, turn))
    scaled0 = mm(inv0, first).astype(BF16)
    fill(FILL[0])
    left1 = (second.astype(F32) - mm(cross, scaled0)).astype(BF16)
    fill(FILL[1])
    scaled1 = mm(inv1, left1)
    fill(FILL[2])
    scaled1_16 = scaled1.astype(BF16)
    spread = mm_tn(jnp.concatenate([first, left1], axis=0), jnp.concatenate([scaled0, scaled1_16], axis=0))
    spread = (spread * inv_snaps).astype(BF16)
    fill(FILL[3])
    fill(len(fillers))
    def make_weights(start, count):
        feats = row_block(start, count)
        weight = (feats.astype(F32) - mm(feats, spread)) * inv_snaps
        inside = min(count, size.packed - start)
        if inside > 0:
            own = panel_w[pl.ds(start, inside), :]
            own = own * jnp.concatenate([diag_col[pl.ds(start, inside), :]] * (snaps // LANES), axis=1)
            if inside < count:
                own = jnp.concatenate([own, jnp.zeros((count - inside, snaps), F32)], axis=0)
            weight = weight - own
        weights[pl.ds(start, count), :] = weight.astype(BF16)

    make_weights(*size.row_blocks[0])
    back = first.astype(F32) - mm_tn(cross, scaled1_16)
    packed = pack(mm(inv0, back.astype(BF16)), scaled1, 0) * inv_snaps
    panel_w[...] = packed
    panel_w16[...] = packed.astype(BF16)
    panel_cols = min(size.packed, size.cols_pad)
    here = pl.ds(0, panel_cols)
    near = column_block(0, panel_cols)
    own = mm(panel_w16[...], near) + schur_q[:, here] * diag_panel[:, here]
    block_own[:, here] = own * jnp.concatenate([diag_col[...]] * (panel_cols // LANES), axis=1)
    weighted = (near.astype(F32) - mm(spread, near)) * inv_snaps
    factor[:, here] = (weighted - panel_w[...].T[:, :panel_cols] * diag_panel[:, here]).astype(BF16)

    delta = row_offset - col_offset

    def write(first_panel):
        used = min(size.packed, cols) if first_panel else 0
        edge = round_up(used, LANES)
        here = pl.ds(0, edge)
        copies = []
        for index, (start, count) in enumerate(size.row_blocks):
            if index + 1 < len(size.row_blocks):
                make_weights(*size.row_blocks[index + 1])
            kept = min(count, rows - start)
            at = pl.ds(start, kept)

            def with_diagonal(values, first_col):
                row_id = lax.broadcasted_iota(jnp.int32, values.shape, 0)
                col_id = lax.broadcasted_iota(jnp.int32, values.shape, 1)
                there = col_id - row_id == delta + (start - first_col)
                return values + jnp.where(there, diag_cols[:, pl.ds(first_col, values.shape[1])], 0.0)

            if used < cols:
                every = column_block(edge, size.cols_pad - edge)
                right = mm(weights[pl.ds(start, count), :], every)[:kept, : cols - edge]
                block_sum[at, pl.ds(edge, cols - edge)] = with_diagonal(right, edge)
            if first_panel:
                left = mm(row_block(start, count), factor[:, here])[:kept, :used]
                inside = min(kept, size.packed - start)
                if inside > 0:
                    mine = block_own[pl.ds(start, inside), pl.ds(0, used)]
                    if inside < kept:
                        mine = jnp.concatenate([mine, jnp.zeros((kept - inside, used), F32)], axis=0)
                    left = left - mine
                block_sum[at, pl.ds(0, used)] = with_diagonal(left, 0)
            copy = pltpu.make_async_copy(block_sum.at[at, :], out.at[at, :], sems.at[index])
            copy.start()
            copies.append(copy)
        for copy in copies:
            copy.wait()

    @pl.when(col_offset == 0)
    def _():
        write(True)

    @pl.when(col_offset != 0)
    def _():
        write(False)


class Sizes:
    def __init__(self, **entries):
        self.__dict__.update(entries)


def eliminate(size, parts, tables, diagonals, known, inverses):
    whole = pl.BlockSpec(memory_space=pltpu.VMEM)
    return pl.pallas_call(
        functools.partial(eliminate_kernel, size, len(parts)),
        in_specs=[whole] * (len(parts) + 17),
        out_specs=pl.BlockSpec(memory_space=pl.ANY),
        out_shape=jax.ShapeDtypeStruct((size.rows, size.cols), F32),
        scratch_shapes=[pltpu.VMEM(shape, BF16) for shape in feature_shapes(size, parts)]
        + [
            pltpu.VMEM((size.rows_feats, size.snaps), BF16),
            pltpu.VMEM((size.packed, size.snaps), F32),
            pltpu.VMEM((size.packed, size.snaps), BF16),
            pltpu.VMEM((size.packed, size.packed), F32),
            pltpu.VMEM((size.packed, size.packed), F32),
            pltpu.VMEM((size.snaps, size.packed), BF16),
            pltpu.VMEM((size.rows, size.cols), F32),
            pltpu.SemaphoreType.DMA((len(size.row_blocks),)),
        ],
        compiler_params=pltpu.CompilerParams(vmem_limit_bytes=VMEM_LIMIT if size.snaps <= 512 else VMEM_LIMIT_LONG),
        name="eliminate",
    )(*parts, *tables, *diagonals, *known, *inverses)


def partner(values, axis, distance):
    count = lax.axis_size(axis)
    return lax.ppermute(values, axis, [(i, i ^ distance) for i in range(count)])


def distances(axis):
    count = lax.axis_size(axis)
    assert count & (count - 1) == 0
    return [1 << bit for bit in range(count.bit_length() - 1)]


def row_blocks(rows):
    return [(start, min(176, rows - start)) for start in range(0, rows, 176)][::-1]


def per_device(codes, node_scale, basis, regular, feature_order, panel_inverse):
    rank = basis.shape[1]
    count = regular.shape[0]
    rows, cols = count // lax.axis_size("node"), count // lax.axis_size("tm")
    snaps = codes.shape[1] * lax.axis_size("tm")
    panels, width = panel_inverse.shape[:2]
    assert panels == 2 and panels * width <= min(rows, cols) and rank == LANES
    shift = width % LANES
    panel_pad = round_up(width + shift, LANES)
    block = 512
    size = Sizes(
        rank=rank,
        snaps=snaps,
        rows=rows,
        cols=cols,
        block=block,
        panel_width=width,
        panel_pad=panel_pad,
        panel_total=panels * width,
        packed=width // LANES * LANES + panel_pad,
        rows_pad=round_up(rows, LANES),
        count=count,
        cols_pad=round_up(cols, LANES),
        chunk=176,
    )
    size.rows_feats = round_up(rows, size.chunk)
    size.row_blocks = row_blocks(size.rows_feats)
    total = project(codes, node_scale, basis)

    gaps = [(0, panel_pad - width)], [(shift, panel_pad - width - shift)]

    made = []
    for turn, distance in enumerate(distances("node")):
        total = total + partner(total, "node", distance)
        if turn == 0:
            total, ready = lax.optimization_barrier((total, prepare_rows(size, feature_order, regular)))
            made += ready
        elif turn == 1:
            ready = prepare_cols(size, feature_order, regular)
            total, ready, panel_inverse = lax.optimization_barrier((total, ready, panel_inverse))
            made += ready
            inverses = [jnp.pad(panel_inverse[k], gaps[k] * 2) for k in range(2)]
        elif turn == 2:
            total, inverses = lax.optimization_barrier((total, inverses))
    lead_r, trail_r, one_r, diag_col, diag_panel, lead_c, trail_c, one_c, diag_cols = made
    tables = (lead_r, trail_r, one_r, lead_c, trail_c, one_c)
    *near, last = distances("tm")
    parts, others = [total], [partner(total, "tm", last)]
    for distance in near:
        parts = parts + [partner(part, "tm", distance) for part in parts]
    known = features(size, parts, tables)
    others, known = lax.optimization_barrier((others, known))
    for distance in near[:-1]:
        others = others + [partner(part, "tm", distance) for part in others]
    rest = [partner(part, "tm", near[-1]) for part in others]
    known = [*known, *features(size, others, tables)]
    return eliminate(size, rest, tables, (diag_col, diag_panel, diag_cols), known, inverses)


def solution(mesh):
    placed = (P("node", "tm"), P("node"), P("node", None), P(), P(), P())
    return jax.shard_map(per_device, mesh=mesh, in_specs=placed, out_specs=P("node", "tm"), check_vma=False)
```
